32 devices in a mesh: side: 2 (over core), grp: 16 (over z, y, x).
Axes of the slice: x: 2, y: 2, z: 4, core: 2. Of those that a mesh axis runs over, the one named last changes fastest.
Arguments:
- query_heads: bfloat16 [256, 8192], P('grp'), may hold values from -160 to 160
- key_cache: bfloat16 [256, 128, 512], P('grp'), may hold values from -4 to 4
- value_cache: bfloat16 [256, 128, 512], P('grp'), may hold values from -6 to 6
- cache_lengths: int32 [256], P('grp'), may hold values from 2 to 128, as said below
- out_weight: bfloat16 [8192, 4096], P(None, 'grp'), may hold values from -0.0625 to 0.0625
- residual: bfloat16 [256, 4096], P('grp'), may hold values from -4 to 4
- norm_gain: float32 [4096], replicated, may hold values from 0.5 to 1.5
- expert_ids: int32 [256, 8], P('grp'), may hold values from 0 to 15, all different within a row; in each aligned block of 16 rows (0 to 15, 16 to 31, ...) at most 16 rows name the same one
- route_weights: float32 [256, 8], P('grp'), may hold values from 0.05 to 0.25
- gate_up: bfloat16 [16, 4096, 1536], P('grp'), may hold values from -0.09375 to 0.09375
- down_weight: bfloat16 [16, 768, 4096], P('grp'), may hold values from -0.21875 to 0.21875
Outputs:
- layer_out: bfloat16 [256, 4096], P('grp', 'side')
The draws below stay inside these ranges and needn't reach their ends.
Inputs may be any that keep to these rules, and one draw needn't show every extreme that they name: `cache_lengths`: at least one session has 128 live positions. `expert_ids`: each row names 8 different experts; among the 16 sessions of one index of grp (aligned blocks of rows) no expert is named by more than 16 rows, a bound that some block reaches.
All inputs are finite; a program needn't handle non-finite values.
Results may differ from the reference program's by a relative error of at most 0.0055.
Values may be sent and summed in bfloat16 or wider, within the bound.
No kernel may reach another device: no remote copies, remote signals or barrier semaphores. Data moves between devices by JAX's collectives and lax.ppermute only.
A program may use at most 128 MiB of HBM per device.

```python
import math
import jax
import jax.numpy as jnp
import numpy as np
from jax import lax

D = 4096
HQ = 64
KVH = 4
HD = 128
HID = 768
TOPK = 8
S_DEV = 16
CTX = 128
SESSIONS = 256
EXPERTS = 16
CAP = 16
N_GRP = 16


def draw_query_heads(key, part):
    fresh_key = jax.random.fold_in(key, 3)
    fresh = jnp.clip(jax.random.normal(fresh_key, (SESSIONS, HQ * HD), jnp.float32), -5.0, 5.0)
    return fresh.astype(jnp.bfloat16)


def draw_key_cache(key, part):
    fresh_key = jax.random.fold_in(key, 5)
    fresh = jnp.clip(jax.random.normal(fresh_key, (SESSIONS, CTX, KVH * HD), jnp.float32), -4.0, 4.0)
    return fresh.astype(jnp.bfloat16)


def draw_cache_lengths(key, part):
    spread = jax.random.randint(jax.random.fold_in(key, 1), (SESSIONS,), 0, CTX - 1)
    factor = jax.random.randint(jax.random.fold_in(key, 2), (SESSIONS // S_DEV,), 1, 5)
    per_session = jnp.repeat(factor, S_DEV)
    lengths = jnp.minimum(2 + spread * per_session // 4, CTX)
    return lengths.at[0].set(CTX).astype(jnp.int32)


def block_levels(own_key, shape, split, low, largest):
    factor_of = 1.0
    for dim, blocks in split:
        steps = jax.random.uniform(jax.random.fold_in(jax.random.fold_in(own_key, 6), dim), (blocks,), jnp.float32, low / len(split), largest / len(split))
        factor_of = factor_of * jnp.repeat(jnp.exp(steps), shape[dim] // blocks).reshape((-1,) + (1,) * (len(shape) - 1 - dim))
    return factor_of


def assign_block(own_key, own, number, rows, number_of, top, most, slope):
    order = jax.random.permutation(own_key, number_of)
    packed, usual = load_shares(number_of, rows * top, most, slope, True), load_shares(number_of, rows * top, most, slope, False)
    places = jnp.arange(number_of)

    def named(tallies, offset_by):
        used = int((tallies > 0).sum())
        fixed = max(1, used // 4)
        shifted = fixed + (places - fixed + offset_by * (used - fixed)) % max(1, number_of - fixed)
        return jnp.zeros((number_of,), jnp.int32).at[order[jnp.where(places < fixed, places, shifted)]].set(jnp.asarray(tallies, jnp.int32))

    tallies = jnp.where(number % 4 == 0, named(packed, number // 4), named(usual, number - number // 4 - 1))
    mixed = jax.random.permutation(jax.random.fold_in(own, 3), number_of)
    source_of, receiver = mixed[0:number_of // 2 * 2:2], mixed[1:number_of // 2 * 2:2]
    room = jnp.minimum(tallies[source_of] - 1, most - tallies[receiver]) // 2
    room = jnp.where((source_of == order[0]) | (receiver == order[0]) | (tallies[receiver] == 0), 0, jnp.maximum(room, 0))
    shifted = jax.random.randint(jax.random.fold_in(own, 4), (number_of // 2,), 0, 1 << 20) % (room + 1)
    tallies = tallies.at[source_of].add(-shifted).at[receiver].add(shifted)
    members = jnp.searchsorted(jnp.cumsum(tallies), jnp.arange(rows * top), side="right").astype(jnp.int32)
    listing = members.reshape(top, rows).T
    listing = listing[jax.random.permutation(jax.random.fold_in(own, 1), rows)]
    offset_by = jax.random.randint(jax.random.fold_in(own, 2), (rows, 1), 0, top)
    return jnp.take_along_axis(listing, (jnp.arange(top)[None, :] + offset_by) % top, axis=1)


def load_shares(amount, total, limit, lean, full):
    weights = [(1 << 20) // math.isqrt(rank ** lean) + 1 for rank in range(1, amount + 1)]
    largest = limit if full else min(limit, max(-(-total // amount), total * weights[0] // sum(weights)))
    least = 1 if total - largest >= amount - 1 else 0
    holding, rest = [largest] + [least] * (amount - 1), total - largest - least * (amount - 1)
    while rest > 0:
        free = [i for i in range(1, amount) if holding[i] < largest] or [i for i in range(1, amount) if holding[i] < limit]
        mass, budget = sum([weights[i] for i in free]), rest
        for i in free:
            more = min(limit - holding[i], max(1, budget * weights[i] // mass), rest)
            holding[i] = holding[i] + more
            rest = rest - more
    return np.array(holding)


def bell_draw(rng, extent, width, bound, pieces=(), held_as=jnp.bfloat16):
    gain = block_levels(rng, extent, pieces, -0.22, 0.18) if pieces else 1.0
    drawn = jax.random.normal(rng, extent, jnp.float32) * width * gain
    return jnp.minimum(jnp.maximum(drawn, -bound), bound).astype(held_as)


def setup_inputs(seed: int = 0) -> dict:
    key_of = jax.random.split(jax.random.key(seed), 12)
    query_heads = draw_query_heads(jax.random.fold_in(key_of[11], 71), 0)
    key_cache = draw_key_cache(jax.random.fold_in(key_of[11], 71), 0)
    value_cache = bell_draw(key_of[2], (SESSIONS, CTX, KVH * HD), 1.0, 6.0, ((0, 16),))
    cache_lengths = draw_cache_lengths(jax.random.fold_in(key_of[11], 71), 0)
    out_weight = bell_draw(key_of[4], (HQ * HD, D), (HQ * HD) ** -0.5, 0.0625, ((1, 16),))
    residual = bell_draw(key_of[5], (SESSIONS, D), 0.5, 4.0, ((0, 16),))
    norm_gain = jnp.clip(1.0 + 0.1 * jax.random.normal(key_of[6], (D,), jnp.float32), 0.5, 1.5)
    expert_ids_keys = jax.random.split(jax.random.fold_in(key_of[7], 1), SESSIONS // S_DEV)
    expert_ids_turns = jax.random.permutation(jax.random.fold_in(key_of[7], 3), SESSIONS // S_DEV)
    expert_ids = jax.vmap(lambda own, number: assign_block(jax.random.fold_in(key_of[7], 2), own, number, S_DEV, EXPERTS, TOPK, CAP, 2))(expert_ids_keys, expert_ids_turns).reshape((SESSIONS, TOPK))
    route_weights = jnp.clip(0.05 + 0.2 * jax.random.uniform(key_of[8], (SESSIONS, TOPK), jnp.float32) ** block_levels(key_of[8], (SESSIONS, TOPK), ((0, 16),), -0.2, 0.2), 0.05, 0.25)
    gate_up = bell_draw(key_of[9], (EXPERTS, D, 2 * HID), D ** -0.5, 0.09375, ((0, 16),))
    down_weight = bell_draw(key_of[10], (EXPERTS, HID, D), HID ** -0.5, 0.21875, ((0, 16),))
    return {"query_heads": query_heads, "key_cache": key_cache, "value_cache": value_cache, "cache_lengths": cache_lengths, "out_weight": out_weight, "residual": residual, "norm_gain": norm_gain, "expert_ids": expert_ids, "route_weights": route_weights, "gate_up": gate_up, "down_weight": down_weight}


def slots_of(expert_block):
    flat_ids = expert_block.reshape(-1).astype(jnp.int32)
    onehot = (flat_ids[:, None] == jnp.arange(EXPERTS, dtype=jnp.int32)[None, :]).astype(jnp.int32)
    running = jnp.cumsum(onehot, axis=0).astype(jnp.int32)
    return (lax.optimization_barrier(jnp.sum(onehot * running, axis=1)) - 1).astype(jnp.int32)

def attend_all(query_heads, key_cache, value_cache, cache_lengths):
    session_count = query_heads.shape[0]
    group_size = HQ // KVH
    queries = query_heads.astype(jnp.float32).reshape(session_count, KVH, group_size, HD)
    key_heads = key_cache.astype(jnp.float32).reshape(session_count, CTX, KVH, HD)
    value_heads = value_cache.astype(jnp.float32).reshape(session_count, CTX, KVH, HD)
    scores = jnp.einsum('skgd,stkd->skgt', queries, key_heads, precision=lax.Precision.HIGHEST) * HD ** (-0.5)
    visible = jnp.arange(CTX, dtype=jnp.int32)[None, :] < cache_lengths.astype(jnp.int32)[:, None]
    scores = jnp.where(visible[:, None, None, :], scores, -1e+30)
    row_max = lax.optimization_barrier(jnp.max(scores, axis=-1, keepdims=True))
    lifted = jnp.exp(scores - row_max)
    softmax_weights = (lifted / lax.optimization_barrier(jnp.sum(lifted, axis=-1, keepdims=True))).astype(jnp.bfloat16)
    attended = jnp.einsum('skgt,stkd->skgd', softmax_weights.astype(jnp.float32), value_heads, precision=lax.Precision.HIGHEST)
    return attended.astype(jnp.bfloat16).reshape(session_count, HQ * HD)

def expert_rows(token_rows, expert_gate_up, expert_down):
    both_halves = jnp.dot(token_rows, expert_gate_up, preferred_element_type=jnp.float32)
    activated = (jax.nn.silu(both_halves[:, :HID]) * both_halves[:, HID:]).astype(jnp.bfloat16)
    return jnp.dot(activated, expert_down, preferred_element_type=jnp.float32).astype(jnp.bfloat16)

def reference(query_heads, key_cache, value_cache, cache_lengths, out_weight, residual, norm_gain, expert_ids, route_weights, gate_up, down_weight):
    attn_out = attend_all(query_heads, key_cache, value_cache, cache_lengths)
    attn_proj = jnp.dot(attn_out, out_weight, preferred_element_type=jnp.float32)
    hidden = residual.astype(jnp.float32) + attn_proj
    scaling = lax.rsqrt(lax.optimization_barrier(jnp.mean(hidden * hidden, axis=-1, keepdims=True)) + 1e-06)
    normed = (hidden * scaling * norm_gain).astype(jnp.bfloat16)
    slot_index = jax.vmap(slots_of)(expert_ids.reshape(N_GRP, S_DEV, TOPK)).reshape(-1).astype(jnp.int32)
    source = jnp.repeat(jnp.arange(N_GRP, dtype=jnp.int32), S_DEV * TOPK)
    expert_flat = expert_ids.reshape(-1).astype(jnp.int32)
    row_index = (source * CAP + slot_index).astype(jnp.int32)
    session = jnp.repeat(jnp.arange(SESSIONS, dtype=jnp.int32), TOPK)
    bucket = jnp.zeros((EXPERTS, N_GRP * CAP, D), jnp.bfloat16).at[expert_flat, row_index].set(normed[session])
    outputs = lax.map(lambda operands: expert_rows(operands[0], operands[1], operands[2]), (bucket, gate_up, down_weight))
    picked = outputs[expert_flat, row_index].astype(jnp.float32).reshape(SESSIONS, TOPK, D)
    mixture = lax.optimization_barrier(jnp.sum(picked * route_weights.astype(jnp.float32)[:, :, None], axis=1))
    return (hidden + mixture).astype(jnp.bfloat16)
```

```python
import functools

import jax
import jax.numpy as jnp
from jax import lax
from jax.experimental import pallas as pl
from jax.experimental.pallas import tpu as pltpu
from jax.sharding import PartitionSpec as P

HQ = 64
KVH = 4
HD = 128
HID = 768
TOPK = 8
CTX = 128
GROUP = HQ // KVH
EPS = 1e-06
CHUNK = 256
LANES = 128
MIB = 1 << 20


CHIPS = 16
PLANES = 4
PAIRS = ((0, 1), (2, 3))
BACK_PAIRS = ((0, 3), (1, 2))
ROUTING = LANES


def exchange(value, bits):
    return lax.ppermute(value, "grp", [(g, g ^ bits) for g in range(CHIPS)])


def piece_order(place, groups):
    if groups != CHIPS:
        return list(range(groups))
    return [place ^ n for n in range(CHIPS)]


def pair_order(place, groups, pairs):
    if groups != CHIPS:
        return list(range(groups))
    return [place ^ (4 * k + f) for pair in pairs for f in range(4) for k in pair]


def after(value, *done):
    return lax.optimization_barrier((value, *done))[0]


def gather(planes):
    own = planes[0]
    z1, z2 = (exchange(planes[k], 4 * k) for k in (1, 2))
    x0, y0 = (exchange(own, f) for f in (1, 2))
    z3 = exchange(after(planes[3], z2), 12)
    x1 = exchange(x0, 4)
    c0 = exchange(y0, 1)
    y1 = exchange(after(z1, y0), 2)
    x2, y2 = (exchange(after(z2, x0, y0, z1), f) for f in (1, 2))
    c1 = exchange(c0, 4)
    c2 = exchange(after(y2, y1, x2, z3), 1)
    d3, x3, y3 = (exchange(after(z3, x1, y1, x2), f) for f in (3, 1, 2))
    return [own, x0, y0, c0, z1, x1, y1, c1, z2, x2, y2, c2, z3, x3, y3, d3]


BY_NEXT_PLANE = (5, 7)


def gather_pairs(piece):
    column = [piece] + [exchange(piece, 4 * k) for k in range(1, PLANES)]
    near, far = (jnp.stack([column[k] for k in pair]) for pair in PAIRS)
    far = after(far, near)
    nears = [exchange(near, f) if f else near for f in range(4)]
    fars = [exchange(far, f) if f else far for f in range(4)]
    return nears, fars


def add(*terms):
    return sum(t.astype(jnp.float32) for t in terms).astype(jnp.bfloat16)


def scatter_sum(first, second):
    first = add(first[0], *[exchange(first[f], f) for f in (3, 1, 2)])
    second = add(second[0], *[exchange(second[f], f) for f in (3, 1, 2)])
    terms = [first[0], exchange(first[1], 12), exchange(second[0], 4), exchange(second[1], 8)]
    return sum(t.astype(jnp.float32) for t in terms)


def attend_kernel(
    planes, ids_hbm, route_hbm, len_hbm, g_hbm, r_hbm, q_hbm, k_hbm, v_hbm, *refs
):
    o_refs = refs[: max(1, planes)]
    gain_ref = refs[max(1, planes)]
    o_ref = o_refs[0]
    len_ref, ids_ref, route_ref, tail_ref, r_ref, q_ref, k_ref, v_ref, sems = refs[-9:]
    side = lax.axis_index("side")
    half = k_ref.shape[0]
    rows = GROUP * half
    depth = HQ * HD // 2
    mine = [side * half + s for s in range(half)]
    small = [
        pltpu.make_async_copy(ids_hbm, ids_ref, sems.at[2 * half + 3]),
        pltpu.make_async_copy(route_hbm, route_ref, sems.at[2 * half + 4]),
    ]
    copies = [
        pltpu.make_async_copy(len_hbm, len_ref, sems.at[2 * half + 1]),
        pltpu.make_async_copy(q_hbm, q_ref, sems.at[2 * half]),
    ]
    copies += [
        pltpu.make_async_copy(k_hbm.at[mine[s]], k_ref.at[s], sems.at[s]) for s in range(half)
    ]
    late = [
        pltpu.make_async_copy(v_hbm.at[mine[s]], v_ref.at[s], sems.at[half + s])
        for s in range(half)
    ]
    late.append(pltpu.make_async_copy(r_hbm, r_ref, sems.at[2 * half + 2]))
    gain = g_hbm.at[lax.axis_index("grp")]
    late.append(pltpu.make_async_copy(gain, gain_ref, sems.at[2 * half + 5]))
    for copy in small + copies + late:
        copy.start()
    session = lax.broadcasted_iota(jnp.int32, (rows, CTX), 0) % half
    place = lax.broadcasted_iota(jnp.int32, (rows, CTX), 1)
    for copy in small:
        copy.wait()
    terms, rest = [], route_ref[...]
    for _ in range(3):
        terms.append(rest.astype(jnp.bfloat16).astype(jnp.float32))
        rest = rest - terms[-1]
    count = 2 * half
    tail_ref[...] = jnp.zeros_like(tail_ref)
    tail_ref[:, :count] = jnp.concatenate(terms[1:], axis=0)
    second = pltpu.roll(tail_ref[...], LANES // 2, axis=1)
    tail_ref[:, :count] = jnp.concatenate([ids_ref[...].astype(jnp.float32), terms[0]], axis=0)
    tail = jnp.where(
        lax.broadcasted_iota(jnp.int32, second.shape, 1) < LANES // 2, tail_ref[...], second
    ).astype(jnp.bfloat16)
    for ref in o_refs:
        ref[:, depth : depth + ROUTING] = tail

    for copy in copies:
        copy.wait()
    lives = [(session == s) & (place < len_ref[mine[s]]) for s in range(half)]
    spreads = []
    for kv in range(KVH):
        parts = []
        for h in range(kv * GROUP, (kv + 1) * GROUP):
            both = q_ref[:, h * HD : (h + 1) * HD].astype(jnp.float32)
            parts.append(jnp.where(side == 0, both[:half], both[half:]))
        queries = jnp.concatenate(parts, axis=0).astype(jnp.bfloat16)
        keys = k_ref[:, :, kv * HD : (kv + 1) * HD].reshape(half * CTX, HD)
        every = lax.dot_general(
            queries, keys, (((1,), (1,)), ((), ())), preferred_element_type=jnp.float32
        )
        scores = jnp.full((rows, CTX), -1e30, jnp.float32)
        for s in range(half):
            part = every[:, s * CTX : (s + 1) * CTX] * HD ** (-0.5)
            scores = jnp.where(lives[s], part, scores)
        lifted = jnp.exp(scores - jnp.max(scores, axis=-1, keepdims=True))
        weights = lifted / jnp.sum(lifted, axis=-1, keepdims=True)
        spreads.append(
            jnp.concatenate(
                [jnp.where(session == s, weights, 0.0).astype(jnp.bfloat16) for s in range(half)],
                axis=1,
            )
        )
    for copy in late:
        copy.wait()
    outs = []
    for kv in range(KVH):
        values = v_ref[:, :, kv * HD : (kv + 1) * HD].reshape(half * CTX, HD)
        outs.append(jnp.dot(spreads[kv], values, preferred_element_type=jnp.float32))
    later = KVH // 2
    for kv in range(later):
        for h in range(GROUP):
            pair = [out[h * half : (h + 1) * half] for out in (outs[kv], outs[kv + later])]
            both = jnp.concatenate(pair, axis=0).astype(jnp.bfloat16)
            for ref in o_refs:
                ref[:, (kv * GROUP + h) * HD : (kv * GROUP + h + 1) * HD] = both
    here = lax.axis_index("grp") // 4
    for k in range(planes):
        wide = r_ref.shape[1] // planes // 2
        parts = []
        for part in range(2):
            start = pl.multiple_of(((here ^ k) * 2 + part) * wide, wide)
            both = r_ref[:, pl.ds(start, wide)].astype(jnp.float32)
            parts.append(jnp.where(side == 0, both[:half], both[half:]))
        tail = jnp.concatenate(parts, axis=0).astype(jnp.bfloat16)
        o_refs[k][:, depth + ROUTING : depth + ROUTING + wide] = tail
        if k == 1:
            o_ref[:, depth + ROUTING + wide :] = tail


def attend(
    groups,
    planes,
    query_heads,
    key_cache,
    value_cache,
    cache_lengths,
    expert_ids,
    route_weights,
    norm_gain,
    residual,
):
    sessions, width = residual.shape
    half = sessions // 2
    columns = width // groups
    hbm_spec = pl.BlockSpec(memory_space=pltpu.HBM)
    vmem_spec = pl.BlockSpec(memory_space=pltpu.VMEM)
    in_hbm = functools.partial(pltpu.with_memory_space_constraint, memory_space=pltpu.HBM)
    outs = max(1, planes)
    tail = width // planes // 2 if planes else 0
    carried = [HQ * HD // 2 + ROUTING + tail * (2 if k == 0 else 1) for k in range(outs)]
    return pl.pallas_call(
        functools.partial(attend_kernel, planes),
        in_specs=[hbm_spec] * 8,
        out_specs=[vmem_spec] * (outs + 1),
        out_shape=[jax.ShapeDtypeStruct((sessions, n), jnp.bfloat16) for n in carried]
        + [jax.ShapeDtypeStruct((1, columns), jnp.float32)],
        scratch_shapes=[
            pltpu.SMEM((sessions,), jnp.int32),
            pltpu.VMEM((TOPK, sessions), jnp.int32),
            pltpu.VMEM((TOPK, sessions), jnp.float32),
            pltpu.VMEM((sessions, ROUTING), jnp.float32),
            pltpu.VMEM((sessions, width), jnp.bfloat16),
            pltpu.VMEM((sessions, HQ * HD), jnp.bfloat16),
            pltpu.VMEM((half, CTX, KVH * HD), jnp.bfloat16),
            pltpu.VMEM((half, CTX, KVH * HD), jnp.bfloat16),
            pltpu.SemaphoreType.DMA((2 * half + 6,)),
        ],
        compiler_params=pltpu.CompilerParams(vmem_limit_bytes=8 * MIB),
        name="attend",
    )(
        in_hbm(expert_ids.T),
        in_hbm(route_weights.T),
        in_hbm(cache_lengths),
        in_hbm(norm_gain.reshape(groups, 1, columns)),
        in_hbm(residual),
        in_hbm(query_heads),
        in_hbm(key_cache),
        in_hbm(value_cache),
    )


def project_kernel(count, waits, *refs):
    refs = refs[waits:]
    pieces = refs[:count]
    *rest, w_ref, g_ref, y_ref, mix_ref, plain = refs[count:]
    blocks, sessions, _ = pieces[0].shape
    depth = w_ref.shape[0] // 2
    half = sessions // 2
    columns = w_ref.shape[1]
    groups = count * blocks
    side, place = lax.axis_index("side"), lax.axis_index("grp")
    order = piece_order(place, groups)
    total = None
    for part in range(2):
        chunk = depth // 4
        for j in range(4):
            a = jnp.concatenate(
                [
                    piece[:, :, j * chunk : (j + 1) * chunk].reshape(blocks * sessions, chunk)
                    for piece in pieces
                ],
                axis=0,
            )
            start = part * depth + j * chunk
            term = jnp.dot(a, w_ref[start : start + chunk], preferred_element_type=jnp.float32)
            got = term if j == 0 else got + term
        got = got.reshape(groups, 2, half, columns)[:, part]
        total = got if total is None else total + got
    own = lax.broadcasted_iota(jnp.int32, (half, LANES), 1) == side * half + (
        lax.broadcasted_iota(jnp.int32, (half, LANES), 0)
    )
    for n in range(count):
        for b in range(blocks):
            span = pl.ds(pl.multiple_of(order[n * blocks + b] * half, half), half)
            value = total[n * blocks + b]
            if not rest:
                start = depth + ROUTING + (2 * columns if n in BY_NEXT_PLANE else 0)
                tail = pieces[n][b, :, start : start + 2 * columns].astype(jnp.float32)
                spot = place % 4
                tail = jnp.where(spot // 2 == 0, tail[:half], tail[half:])
                value = value + jnp.where(spot % 2 == 0, tail[:, :columns], tail[:, columns:])
            plain[span, :] = value
            first = pieces[n][b, :, depth : depth + ROUTING].astype(jnp.float32)
            second = pltpu.roll(first, LANES // 2, axis=1)
            weights = first[half:] + (second[:half] + second[half:])
            chosen = jnp.where(first[:half] == place.astype(jnp.float32), weights, 0.0)
            chosen = jnp.sum(chosen, axis=0, keepdims=True)
            mix_ref[span, :] = jnp.sum(jnp.where(own, chosen, 0.0), axis=1, keepdims=True)
    hidden = plain[...]
    if rest:
        hidden = hidden + rest[0][...].astype(jnp.float32)
    y_ref[...] = (hidden * g_ref[...]).astype(jnp.bfloat16)


def project(pieces, out_weight, gain_columns, residual_columns=None, waits=()):
    count = len(pieces)
    columns = out_weight.shape[1]
    rows = sum(p.shape[0] for p in pieces) * pieces[0].shape[1] // 2
    rest = [] if residual_columns is None else [residual_columns]
    vmem_spec = pl.BlockSpec(memory_space=pltpu.VMEM)
    return pl.pallas_call(
        functools.partial(project_kernel, count, len(waits)),
        in_specs=[pl.BlockSpec(memory_space=pl.ANY)] * len(waits)
        + [vmem_spec] * (count + len(rest) + 2),
        out_specs=[vmem_spec] * 2,
        out_shape=[
            jax.ShapeDtypeStruct((rows, columns), jnp.bfloat16),
            jax.ShapeDtypeStruct((rows, 1), jnp.float32),
        ],
        scratch_shapes=[pltpu.VMEM((rows, columns), jnp.float32)],
        compiler_params=pltpu.CompilerParams(vmem_limit_bytes=8 * MIB),
        name="project",
    )(
        *waits,
        *pieces,
        *rest,
        pltpu.with_memory_space_constraint(out_weight, pltpu.VMEM),
        gain_columns,
    )


def take_chunk(store, g_ref, plain, hid_ref, chunk, chunks):
    side, place = lax.axis_index("side"), lax.axis_index("grp")
    value = store.astype(jnp.float32) * (1.0 / g_ref[chunk])
    plain[...] = value
    local, late = chunk % (chunks // 2), chunk // (chunks // 2)
    rows = pl.ds(pl.multiple_of(8 * ((side + late) % 2), 8), 8)
    columns = pl.ds(pl.multiple_of(local * CHUNK, CHUNK), CHUNK)
    hid_ref[rows, columns] = plain[pl.ds(pl.multiple_of(place * 8, 8), 8), :]
    squares = value * value
    return squares[:, :LANES] + squares[:, LANES:]


def weight_copies(gu_hbm, dst, sems, first):
    return [
        pltpu.make_async_copy(
            gu_hbm.at[0, pl.ds(pl.multiple_of((first + j) * CHUNK, CHUNK), CHUNK)],
            dst.at[pl.ds(j * CHUNK, CHUNK)],
            sems.at[j],
        )
        for j in range(dst.shape[0] // CHUNK)
    ]


def stage_kernel(_, gu_hbm, weights, done, sems):
    own = weights.shape[0] // CHUNK
    copies = weight_copies(
        gu_hbm, weights, sems, (lax.axis_index("grp") // (CHIPS // 2)) * own
    )
    for copy in copies:
        copy.start()
    done[...] = jnp.zeros_like(done)
    for copy in copies:
        copy.wait()


def stage(gate_up, arrived):
    half = gate_up.shape[1] // 2
    hbm_spec = pl.BlockSpec(memory_space=pltpu.HBM)
    vmem_spec = pl.BlockSpec(memory_space=pltpu.VMEM)
    return pl.pallas_call(
        stage_kernel,
        in_specs=[pl.BlockSpec(memory_space=pl.ANY), hbm_spec],
        out_specs=[vmem_spec] * 2,
        out_shape=[
            jax.ShapeDtypeStruct((half, 2 * HID), jnp.bfloat16),
            jax.ShapeDtypeStruct((8, LANES), jnp.float32),
        ],
        scratch_shapes=[pltpu.SemaphoreType.DMA((half // CHUNK,))],
        compiler_params=pltpu.CompilerParams(vmem_limit_bytes=2 * MIB),
        cost_estimate=pl.CostEstimate(
            flops=0, bytes_accessed=half * 4 * HID, transcendentals=0
        ),
        name="stage",
    )(arrived, pltpu.with_memory_space_constraint(gate_up, pltpu.HBM))


def near_kernel(count, *refs):
    pieces = refs[:count]
    weights, gu_hbm, g_ref, acc, sq_ref, hid_ref, kept, store, plain, sems = refs[count:]
    place = lax.axis_index("grp")
    chunks = g_ref.shape[0]
    own = chunks // 2
    first = (place // (CHIPS // 2)) * own
    copies = weight_copies(gu_hbm, kept, sems, own - first)
    for copy in copies:
        copy.start()
    order = pair_order(place, CHIPS, PAIRS)[:own]
    squares = jnp.zeros(sq_ref.shape, jnp.float32)
    for n in range(count):
        for b in range(2):
            chunk = order[2 * n + b]
            piece = pieces[n][b]
            store[chunk - first] = piece
            squares += take_chunk(piece, g_ref, plain, hid_ref, chunk, chunks)
    sq_ref[...] = squares
    y = jnp.concatenate([store[j] for j in range(own)], axis=1)
    for n in range(2 * HID // CHUNK):
        cols = slice(n * CHUNK, (n + 1) * CHUNK)
        acc[:, cols] = jnp.dot(y, weights[:, cols], preferred_element_type=jnp.float32)
    for copy in copies:
        copy.wait()


def near(pieces, staged, gate_up, norm_gain):
    rows = pieces[0].shape[1]
    width = gate_up.shape[1]
    chunks = width // CHUNK
    vmem_spec = pl.BlockSpec(memory_space=pltpu.VMEM)
    hbm_spec = pl.BlockSpec(memory_space=pltpu.HBM)
    count = len(pieces)
    return pl.pallas_call(
        functools.partial(near_kernel, count),
        in_specs=[vmem_spec] * (count + 1) + [hbm_spec, vmem_spec],
        out_specs=[vmem_spec] * 4,
        out_shape=[
            jax.ShapeDtypeStruct((rows, 2 * HID), jnp.float32),
            jax.ShapeDtypeStruct((rows, LANES), jnp.float32),
            jax.ShapeDtypeStruct((16, width // 2), jnp.float32),
            jax.ShapeDtypeStruct((width // 2, 2 * HID), jnp.bfloat16),
        ],
        scratch_shapes=[
            pltpu.VMEM((chunks // 2, rows, CHUNK), jnp.bfloat16),
            pltpu.VMEM((rows, CHUNK), jnp.float32),
            pltpu.SemaphoreType.DMA((chunks // 2,)),
        ],
        compiler_params=pltpu.CompilerParams(vmem_limit_bytes=6 * MIB),
        cost_estimate=pl.CostEstimate(
            flops=2 * rows * width * HID, bytes_accessed=width * 4 * HID, transcendentals=0
        ),
        name="near",
    )(
        *pieces,
        pltpu.with_memory_space_constraint(staged, pltpu.VMEM),
        pltpu.with_memory_space_constraint(gate_up, pltpu.HBM),
        norm_gain.reshape(chunks, 1, CHUNK),
    )


def expert_kernel(count, outs, resumed, *refs):
    pieces = refs[:count]
    gu_ref, dn_ref, g_ref, mix_ref = refs[count : count + 4]
    rest = refs[count + 4 :]
    if resumed:
        acc_ref, sq_ref, old_ref = rest[:3]
        rest = rest[3:]
    o_refs, (hid_ref, store, plain, first, second) = rest[:outs], rest[outs:]
    side, place = lax.axis_index("side"), lax.axis_index("grp")
    own, rows, _ = store.shape
    chunks = g_ref.shape[0]
    width = chunks * CHUNK
    groups = rows // 8
    blocks = groups // outs
    spans = pieces[0].shape[0]
    back = pair_order(place, groups, BACK_PAIRS)
    if resumed:
        order = pair_order(place, groups, PAIRS)[own:]
        base = own - (place // (CHIPS // 2)) * own
        squares = sq_ref[...]
        hid_ref[...] = old_ref[...]
    else:
        order, base = list(range(chunks)), 0
        squares = jnp.zeros((rows, LANES), jnp.float32)
    for n in range(count):
        for b in range(spans):
            chunk = order[n * spans + b]
            piece = pieces[n][b]
            store[chunk - base] = piece
            squares += take_chunk(piece, g_ref, plain, hid_ref, chunk, chunks)
    mean = jnp.sum(squares, axis=-1, keepdims=True) * (1.0 / width)
    scaling = lax.rsqrt(mean + EPS)
    y = jnp.concatenate([store[j] for j in range(own)], axis=1)
    activated = []
    for n in range(HID // CHUNK):
        halves = []
        for start in (0, HID):
            cols = slice(start + n * CHUNK, start + (n + 1) * CHUNK)
            value = jnp.dot(y, gu_ref[:, cols], preferred_element_type=jnp.float32)
            if resumed:
                value = value + acc_ref[:, cols]
            halves.append(value * scaling)
        gate, up = halves
        activated.append((gate / (1.0 + jnp.exp(-gate)) * up).astype(jnp.bfloat16))
    activated = jnp.concatenate(activated, axis=1)
    mix = mix_ref[...]
    wide = width // 8
    for j in range(4):
        results = [
            jnp.dot(
                activated,
                dn_ref[0, :, start + j * wide : start + (j + 1) * wide],
                preferred_element_type=jnp.float32,
            )
            * mix
            for start in (0, width // 2)
        ]
        first[...] = jnp.where(side == 0, results[0], results[1])
        second[...] = jnp.where(side == 0, results[1], results[0])
        for n in range(outs):
            for b in range(blocks):
                span = pl.ds(pl.multiple_of(back[n * blocks + b] * 8, 8), 8)
                o_refs[n][b, :, j * wide : (j + 1) * wide] = jnp.concatenate(
                    [first[span, :], second[span, :]], axis=0
                ).astype(jnp.bfloat16)


def experts(pieces, gate_up, down_weight, norm_gain, mix, outs, begun=()):
    rows = mix.shape[0]
    width = down_weight.shape[2]
    chunks = width // CHUNK
    groups = rows // 8
    vmem_spec = pl.BlockSpec(memory_space=pltpu.VMEM)
    count = len(pieces)
    in_vmem = functools.partial(pltpu.with_memory_space_constraint, memory_space=pltpu.VMEM)
    return pl.pallas_call(
        functools.partial(expert_kernel, count, outs, bool(begun)),
        in_specs=[vmem_spec] * (count + 4 + len(begun)),
        out_specs=[vmem_spec] * (outs + 1),
        out_shape=[jax.ShapeDtypeStruct((groups // outs, 16, width // 2), jnp.bfloat16)] * outs
        + [jax.ShapeDtypeStruct((16, width // 2), jnp.float32)],
        scratch_shapes=[
            pltpu.VMEM((gate_up.shape[0] // CHUNK, rows, CHUNK), jnp.bfloat16),
            pltpu.VMEM((rows, CHUNK), jnp.float32),
            pltpu.VMEM((rows, width // 8), jnp.float32),
            pltpu.VMEM((rows, width // 8), jnp.float32),
        ],
        compiler_params=pltpu.CompilerParams(vmem_limit_bytes=(8 if rows <= 128 else 24) * MIB),
        name="experts",
    )(
        *pieces,
        in_vmem(gate_up),
        in_vmem(down_weight),
        norm_gain.reshape(chunks, 1, CHUNK),
        mix,
        *begun,
    )


def body(
    query_heads,
    key_cache,
    value_cache,
    cache_lengths,
    out_weight,
    residual,
    norm_gain,
    expert_ids,
    route_weights,
    gate_up,
    down_weight,
):
    side = lax.axis_index("side")
    groups = lax.axis_size("grp")
    sessions, width = residual.shape
    half = sessions // 2
    rows = groups * half
    columns = width // groups
    arrays = (
        query_heads,
        key_cache,
        value_cache,
        cache_lengths,
        expert_ids,
        route_weights,
        norm_gain,
        residual,
    )
    if groups == CHIPS:
        *carried, gain = attend(groups, PLANES, *arrays)
        pieces = gather(carried)
        staged, done = stage(gate_up, pieces[11])
        y, mix = project([p[None] for p in pieces], out_weight, gain, waits=(done,))
        nears, fars = gather_pairs(y)
        *begun, kept = near(nears, staged, gate_up, norm_gain)
        *sums, hidden = experts(fars, kept, down_weight, norm_gain, mix, 8, begun)
        mixture = scatter_sum(sums[:4], sums[4:])
    else:
        own_residual = lax.dynamic_slice_in_dim(residual, side * half, half, axis=0)
        residual_columns = lax.all_to_all(
            own_residual.reshape(half, groups, columns).transpose(1, 0, 2),
            "grp",
            split_axis=0,
            concat_axis=0,
            tiled=True,
        ).reshape(rows, columns)
        attn_out, gain = attend(groups, 0, *arrays)
        pieces = lax.all_gather(attn_out, "grp", axis=0)
        y, mix = project([pieces], out_weight, gain, residual_columns)
        y_all = lax.all_gather(y, "grp", axis=0).transpose(1, 0, 2)
        y_chunks = y_all.reshape(rows, width // CHUNK, CHUNK).transpose(1, 0, 2)
        *sums, hidden = experts([y_chunks], gate_up[0], down_weight, norm_gain, mix, 1)
        sent = lax.all_to_all(sums[0], "grp", split_axis=0, concat_axis=0, tiled=True)
        mixture = jnp.sum(sent.astype(jnp.float32), axis=0)
    ready = (hidden + mixture).astype(jnp.bfloat16)
    mine, other = ready[:half], ready[half:]
    other = lax.ppermute(other, "side", [(0, 1), (1, 0)])
    return jnp.where(
        side == 0, jnp.concatenate([mine, other]), jnp.concatenate([other, mine])
    )


def solution(mesh):
    return jax.shard_map(
        body,
        mesh=mesh,
        in_specs=(
            P("grp", None),
            P("grp", None, None),
            P("grp", None, None),
            P("grp"),
            P(None, "grp"),
            P("grp", None),
            P(),
            P("grp", None),
            P("grp", None),
            P("grp", None, None),
            P("grp", None, None),
        ),
        out_specs=P("grp", "side"),
        check_vma=False,
    )
```

```python
import functools

import jax
import jax.numpy as jnp
from jax import lax
from jax.experimental import pallas as pl
from jax.experimental.pallas import tpu as pltpu
from jax.sharding import PartitionSpec as P

HQ = 64
KVH = 4
HD = 128
HID = 768
TOPK = 8
CTX = 128
GROUP = HQ // KVH
EPS = 1e-06
CHUNK = 256
LANES = 128
MIB = 1 << 20


CHIPS = 16
PLANES = 4
PAIRS = ((0, 1), (2, 3))
BACK_PAIRS = ((2, 3), (0, 1))
ROUTING = LANES


def exchange(value, bits):
    return lax.ppermute(value, "grp", [(g, g ^ bits) for g in range(CHIPS)])


def piece_order(place, groups):
    if groups != CHIPS:
        return list(range(groups))
    return [place ^ n for n in range(CHIPS)]


def pair_order(place, groups, pairs):
    if groups != CHIPS:
        return list(range(groups))
    return [place ^ (4 * k + f) for pair in pairs for f in range(4) for k in pair]


def after(value, *done):
    return lax.optimization_barrier((value, *done))[0]


def gather(planes):
    own = planes[0]
    z1, z2 = (exchange(planes[k], 4 * k) for k in (1, 2))
    x0, y0 = (exchange(own, f) for f in (1, 2))
    z3 = exchange(after(planes[3], z1), 12)
    x1 = exchange(x0, 4)
    c0 = exchange(y0, 1)
    y1 = exchange(after(z1, y0), 2)
    x2, y2 = (exchange(z2, f) for f in (1, 2))
    c1 = exchange(c0, 4)
    c2 = exchange(after(y2, y1), 1)
    d3, x3, y3 = (exchange(after(z3, x1, y1, x2), f) for f in (3, 1, 2))
    return [own, x0, y0, c0, z1, x1, y1, c1, z2, x2, y2, c2, z3, x3, y3, d3]


BY_NEXT_PLANE = (5, 7)


def gather_pairs(piece):
    column = [piece] + [exchange(piece, 4 * k) for k in range(1, PLANES)]
    near, far = (jnp.stack([column[k] for k in pair]) for pair in PAIRS)
    far = after(far, near)
    nears = [exchange(near, f) if f else near for f in range(4)]
    fars = [exchange(far, f) if f else far for f in range(4)]
    return nears, fars


def add(*terms):
    return sum(t.astype(jnp.float32) for t in terms).astype(jnp.bfloat16)


def scatter_sum(far, near):
    far = add(far[0], *[exchange(far[f], f) for f in (3, 1, 2)])
    near = add(near[0], *[exchange(near[f], f) for f in (3, 1, 2)])
    late = exchange(far[0], 8).astype(jnp.float32) + exchange(far[1], 12).astype(jnp.float32)
    late = lax.optimization_barrier(late)
    return near[0].astype(jnp.float32) + exchange(near[1], 4).astype(jnp.float32) + late


def attend_kernel(
    planes, ids_hbm, route_hbm, len_hbm, g_hbm, r_hbm, q_hbm, k_hbm, v_hbm, *refs
):
    o_refs = refs[: max(1, planes)]
    gain_ref = refs[max(1, planes)]
    o_ref = o_refs[0]
    len_ref, ids_ref, route_ref, tail_ref, r_ref, q_ref, k_ref, v_ref, sems = refs[-9:]
    side = lax.axis_index("side")
    half = k_ref.shape[0]
    rows = GROUP * half
    depth = HQ * HD // 2
    mine = [side * half + s for s in range(half)]
    small = [
        pltpu.make_async_copy(ids_hbm, ids_ref, sems.at[2 * half + 3]),
        pltpu.make_async_copy(route_hbm, route_ref, sems.at[2 * half + 4]),
    ]
    copies = [
        pltpu.make_async_copy(len_hbm, len_ref, sems.at[2 * half + 1]),
        pltpu.make_async_copy(q_hbm, q_ref, sems.at[2 * half]),
    ]
    copies += [
        pltpu.make_async_copy(k_hbm.at[mine[s]], k_ref.at[s], sems.at[s]) for s in range(half)
    ]
    late = [
        pltpu.make_async_copy(v_hbm.at[mine[s]], v_ref.at[s], sems.at[half + s])
        for s in range(half)
    ]
    late.append(pltpu.make_async_copy(r_hbm, r_ref, sems.at[2 * half + 2]))
    gain = g_hbm.at[lax.axis_index("grp")]
    late.append(pltpu.make_async_copy(gain, gain_ref, sems.at[2 * half + 5]))
    for copy in small + copies + late:
        copy.start()
    session = lax.broadcasted_iota(jnp.int32, (rows, CTX), 0) % half
    place = lax.broadcasted_iota(jnp.int32, (rows, CTX), 1)
    for copy in small:
        copy.wait()
    terms, rest = [], route_ref[...]
    for _ in range(3):
        terms.append(rest.astype(jnp.bfloat16).astype(jnp.float32))
        rest = rest - terms[-1]
    count = 2 * half
    tail_ref[...] = jnp.zeros_like(tail_ref)
    tail_ref[:, :count] = jnp.concatenate(terms[1:], axis=0)
    second = pltpu.roll(tail_ref[...], LANES // 2, axis=1)
    tail_ref[:, :count] = jnp.concatenate([ids_ref[...].astype(jnp.float32), terms[0]], axis=0)
    tail = jnp.where(
        lax.broadcasted_iota(jnp.int32, second.shape, 1) < LANES // 2, tail_ref[...], second
    ).astype(jnp.bfloat16)
    for ref in o_refs:
        ref[:, depth : depth + ROUTING] = tail

    for copy in copies:
        copy.wait()
    lives = [(session == s) & (place < len_ref[mine[s]]) for s in range(half)]
    spreads = []
    for kv in range(KVH):
        parts = []
        for h in range(kv * GROUP, (kv + 1) * GROUP):
            both = q_ref[:, h * HD : (h + 1) * HD].astype(jnp.float32)
            parts.append(jnp.where(side == 0, both[:half], both[half:]))
        queries = jnp.concatenate(parts, axis=0).astype(jnp.bfloat16)
        keys = k_ref[:, :, kv * HD : (kv + 1) * HD].reshape(half * CTX, HD)
        every = lax.dot_general(
            queries, keys, (((1,), (1,)), ((), ())), preferred_element_type=jnp.float32
        )
        scores = jnp.full((rows, CTX), -1e30, jnp.float32)
        for s in range(half):
            part = every[:, s * CTX : (s + 1) * CTX] * HD ** (-0.5)
            scores = jnp.where(lives[s], part, scores)
        lifted = jnp.exp(scores - jnp.max(scores, axis=-1, keepdims=True))
        weights = lifted / jnp.sum(lifted, axis=-1, keepdims=True)
        spreads.append(
            jnp.concatenate(
                [jnp.where(session == s, weights, 0.0).astype(jnp.bfloat16) for s in range(half)],
                axis=1,
            )
        )
    for copy in late:
        copy.wait()
    outs = []
    for kv in range(KVH):
        values = v_ref[:, :, kv * HD : (kv + 1) * HD].reshape(half * CTX, HD)
        outs.append(jnp.dot(spreads[kv], values, preferred_element_type=jnp.float32))
    later = KVH // 2
    for kv in range(later):
        for h in range(GROUP):
            pair = [out[h * half : (h + 1) * half] for out in (outs[kv], outs[kv + later])]
            both = jnp.concatenate(pair, axis=0).astype(jnp.bfloat16)
            for ref in o_refs:
                ref[:, (kv * GROUP + h) * HD : (kv * GROUP + h + 1) * HD] = both
    here = lax.axis_index("grp") // 4
    for k in range(planes):
        wide = r_ref.shape[1] // planes // 2
        parts = []
        for part in range(2):
            start = pl.multiple_of(((here ^ k) * 2 + part) * wide, wide)
            both = r_ref[:, pl.ds(start, wide)].astype(jnp.float32)
            parts.append(jnp.where(side == 0, both[:half], both[half:]))
        tail = jnp.concatenate(parts, axis=0).astype(jnp.bfloat16)
        o_refs[k][:, depth + ROUTING : depth + ROUTING + wide] = tail
        if k == 1:
            o_ref[:, depth + ROUTING + wide :] = tail


def attend(
    groups,
    planes,
    query_heads,
    key_cache,
    value_cache,
    cache_lengths,
    expert_ids,
    route_weights,
    norm_gain,
    residual,
):
    sessions, width = residual.shape
    half = sessions // 2
    columns = width // groups
    hbm_spec = pl.BlockSpec(memory_space=pltpu.HBM)
    vmem_spec = pl.BlockSpec(memory_space=pltpu.VMEM)
    in_hbm = functools.partial(pltpu.with_memory_space_constraint, memory_space=pltpu.HBM)
    outs = max(1, planes)
    tail = width // planes // 2 if planes else 0
    carried = [HQ * HD // 2 + ROUTING + tail * (2 if k == 0 else 1) for k in range(outs)]
    return pl.pallas_call(
        functools.partial(attend_kernel, planes),
        in_specs=[hbm_spec] * 8,
        out_specs=[vmem_spec] * (outs + 1),
        out_shape=[jax.ShapeDtypeStruct((sessions, n), jnp.bfloat16) for n in carried]
        + [jax.ShapeDtypeStruct((1, columns), jnp.float32)],
        scratch_shapes=[
            pltpu.SMEM((sessions,), jnp.int32),
            pltpu.VMEM((TOPK, sessions), jnp.int32),
            pltpu.VMEM((TOPK, sessions), jnp.float32),
            pltpu.VMEM((sessions, ROUTING), jnp.float32),
            pltpu.VMEM((sessions, width), jnp.bfloat16),
            pltpu.VMEM((sessions, HQ * HD), jnp.bfloat16),
            pltpu.VMEM((half, CTX, KVH * HD), jnp.bfloat16),
            pltpu.VMEM((half, CTX, KVH * HD), jnp.bfloat16),
            pltpu.SemaphoreType.DMA((2 * half + 6,)),
        ],
        compiler_params=pltpu.CompilerParams(vmem_limit_bytes=8 * MIB),
        name="attend",
    )(
        in_hbm(expert_ids.T),
        in_hbm(route_weights.T),
        in_hbm(cache_lengths),
        in_hbm(norm_gain.reshape(groups, 1, columns)),
        in_hbm(residual),
        in_hbm(query_heads),
        in_hbm(key_cache),
        in_hbm(value_cache),
    )


def project_kernel(count, waits, *refs):
    refs = refs[waits:]
    pieces = refs[:count]
    *rest, w_ref, g_ref, y_ref, mix_ref, plain = refs[count:]
    blocks, sessions, _ = pieces[0].shape
    depth = w_ref.shape[0] // 2
    half = sessions // 2
    columns = w_ref.shape[1]
    groups = count * blocks
    side, place = lax.axis_index("side"), lax.axis_index("grp")
    order = piece_order(place, groups)
    total = None
    for part in range(2):
        chunk = depth // 4
        for j in range(4):
            a = jnp.concatenate(
                [
                    piece[:, :, j * chunk : (j + 1) * chunk].reshape(blocks * sessions, chunk)
                    for piece in pieces
                ],
                axis=0,
            )
            start = part * depth + j * chunk
            term = jnp.dot(a, w_ref[start : start + chunk], preferred_element_type=jnp.float32)
            got = term if j == 0 else got + term
        got = got.reshape(groups, 2, half, columns)[:, part]
        total = got if total is None else total + got
    own = lax.broadcasted_iota(jnp.int32, (half, LANES), 1) == side * half + (
        lax.broadcasted_iota(jnp.int32, (half, LANES), 0)
    )
    for n in range(count):
        for b in range(blocks):
            span = pl.ds(pl.multiple_of(order[n * blocks + b] * half, half), half)
            value = total[n * blocks + b]
            if not rest:
                start = depth + ROUTING + (2 * columns if n in BY_NEXT_PLANE else 0)
                tail = pieces[n][b, :, start : start + 2 * columns].astype(jnp.float32)
                spot = place % 4
                tail = jnp.where(spot // 2 == 0, tail[:half], tail[half:])
                value = value + jnp.where(spot % 2 == 0, tail[:, :columns], tail[:, columns:])
            plain[span, :] = value
            first = pieces[n][b, :, depth : depth + ROUTING].astype(jnp.float32)
            second = pltpu.roll(first, LANES // 2, axis=1)
            weights = first[half:] + (second[:half] + second[half:])
            chosen = jnp.where(first[:half] == place.astype(jnp.float32), weights, 0.0)
            chosen = jnp.sum(chosen, axis=0, keepdims=True)
            mix_ref[span, :] = jnp.sum(jnp.where(own, chosen, 0.0), axis=1, keepdims=True)
    hidden = plain[...]
    if rest:
        hidden = hidden + rest[0][...].astype(jnp.float32)
    y_ref[...] = (hidden * g_ref[...]).astype(jnp.bfloat16)


def project(pieces, out_weight, gain_columns, residual_columns=None, waits=()):
    count = len(pieces)
    columns = out_weight.shape[1]
    rows = sum(p.shape[0] for p in pieces) * pieces[0].shape[1] // 2
    rest = [] if residual_columns is None else [residual_columns]
    vmem_spec = pl.BlockSpec(memory_space=pltpu.VMEM)
    return pl.pallas_call(
        functools.partial(project_kernel, count, len(waits)),
        in_specs=[pl.BlockSpec(memory_space=pl.ANY)] * len(waits)
        + [vmem_spec] * (count + len(rest) + 2),
        out_specs=[vmem_spec] * 2,
        out_shape=[
            jax.ShapeDtypeStruct((rows, columns), jnp.bfloat16),
            jax.ShapeDtypeStruct((rows, 1), jnp.float32),
        ],
        scratch_shapes=[pltpu.VMEM((rows, columns), jnp.float32)],
        compiler_params=pltpu.CompilerParams(vmem_limit_bytes=8 * MIB),
        name="project",
    )(
        *waits,
        *pieces,
        *rest,
        pltpu.with_memory_space_constraint(out_weight, pltpu.VMEM),
        gain_columns,
    )


def take_chunk(store, g_ref, plain, hid_ref, chunk, chunks):
    side, place = lax.axis_index("side"), lax.axis_index("grp")
    value = store.astype(jnp.float32) * (1.0 / g_ref[chunk])
    plain[...] = value
    local, late = chunk % (chunks // 2), chunk // (chunks // 2)
    rows = pl.ds(pl.multiple_of(8 * ((side + late) % 2), 8), 8)
    columns = pl.ds(pl.multiple_of(local * CHUNK, CHUNK), CHUNK)
    hid_ref[rows, columns] = plain[pl.ds(pl.multiple_of(place * 8, 8), 8), :]
    squares = value * value
    return squares[:, :LANES] + squares[:, LANES:]


def stage_kernel(_, gu_hbm, weights, done, sems):
    copies = [
        pltpu.make_async_copy(
            gu_hbm.at[0, pl.ds(j * CHUNK, CHUNK)], weights.at[pl.ds(j * CHUNK, CHUNK)], sems.at[j]
        )
        for j in range(weights.shape[0] // CHUNK)
    ]
    for copy in copies:
        copy.start()
    done[...] = jnp.zeros_like(done)
    for copy in copies:
        copy.wait()


def stage(gate_up, arrived):
    depth = gate_up.shape[1]
    hbm_spec = pl.BlockSpec(memory_space=pltpu.HBM)
    vmem_spec = pl.BlockSpec(memory_space=pltpu.VMEM)
    return pl.pallas_call(
        stage_kernel,
        in_specs=[pl.BlockSpec(memory_space=pl.ANY), hbm_spec],
        out_specs=[vmem_spec] * 2,
        out_shape=[
            jax.ShapeDtypeStruct((depth, 2 * HID), jnp.bfloat16),
            jax.ShapeDtypeStruct((8, LANES), jnp.float32),
        ],
        scratch_shapes=[pltpu.SemaphoreType.DMA((depth // CHUNK,))],
        compiler_params=pltpu.CompilerParams(vmem_limit_bytes=2 * MIB),
        cost_estimate=pl.CostEstimate(
            flops=0, bytes_accessed=depth * 4 * HID, transcendentals=0
        ),
        name="stage",
    )(arrived, pltpu.with_memory_space_constraint(gate_up, pltpu.HBM))


def near_kernel(count, *refs):
    pieces = refs[:count]
    weights, g_ref, acc, sq_ref, hid_ref, store, plain = refs[count:]
    place = lax.axis_index("grp")
    chunks = g_ref.shape[0]
    own = chunks // 2
    first = (place // (CHIPS // 2)) * own
    order = pair_order(place, CHIPS, PAIRS)[:own]
    mine = weights.at[pl.ds(pl.multiple_of(first * CHUNK, CHUNK), own * CHUNK)]
    squares = jnp.zeros(sq_ref.shape, jnp.float32)
    for n in range(count):
        for b in range(2):
            chunk = order[2 * n + b]
            piece = pieces[n][b]
            store[chunk - first] = piece
            squares += take_chunk(piece, g_ref, plain, hid_ref, chunk, chunks)
    sq_ref[...] = squares
    y = jnp.concatenate([store[j] for j in range(own)], axis=1)
    for n in range(2 * HID // CHUNK):
        cols = slice(n * CHUNK, (n + 1) * CHUNK)
        acc[:, cols] = jnp.dot(y, mine[:, cols], preferred_element_type=jnp.float32)


def near(pieces, staged, norm_gain):
    rows = pieces[0].shape[1]
    width = staged.shape[0]
    chunks = width // CHUNK
    vmem_spec = pl.BlockSpec(memory_space=pltpu.VMEM)
    count = len(pieces)
    return pl.pallas_call(
        functools.partial(near_kernel, count),
        in_specs=[vmem_spec] * (count + 2),
        out_specs=[vmem_spec] * 3,
        out_shape=[
            jax.ShapeDtypeStruct((rows, 2 * HID), jnp.float32),
            jax.ShapeDtypeStruct((rows, LANES), jnp.float32),
            jax.ShapeDtypeStruct((16, width // 2), jnp.float32),
        ],
        scratch_shapes=[
            pltpu.VMEM((chunks // 2, rows, CHUNK), jnp.bfloat16),
            pltpu.VMEM((rows, CHUNK), jnp.float32),
        ],
        compiler_params=pltpu.CompilerParams(vmem_limit_bytes=6 * MIB),
        cost_estimate=pl.CostEstimate(
            flops=2 * rows * width * HID, bytes_accessed=width * 4 * HID, transcendentals=0
        ),
        name="near",
    )(
        *pieces,
        pltpu.with_memory_space_constraint(staged, pltpu.VMEM),
        norm_gain.reshape(chunks, 1, CHUNK),
    )


def expert_kernel(count, outs, resumed, *refs):
    pieces = refs[:count]
    gu_ref, dn_ref, g_ref, mix_ref = refs[count : count + 4]
    rest = refs[count + 4 :]
    if resumed:
        acc_ref, sq_ref, old_ref = rest[:3]
        rest = rest[3:]
    o_refs, (hid_ref, store, plain, first, second) = rest[:outs], rest[outs:]
    side, place = lax.axis_index("side"), lax.axis_index("grp")
    own, rows, _ = store.shape
    chunks = g_ref.shape[0]
    width = chunks * CHUNK
    groups = rows // 8
    blocks = groups // outs
    spans = pieces[0].shape[0]
    back = pair_order(place, groups, BACK_PAIRS)
    if resumed:
        order = pair_order(place, groups, PAIRS)[own:]
        base = own - (place // (CHIPS // 2)) * own
        gu_ref = gu_ref.at[pl.ds(pl.multiple_of(base * CHUNK, CHUNK), own * CHUNK)]
        squares = sq_ref[...]
        hid_ref[...] = old_ref[...]
    else:
        order, base = list(range(chunks)), 0
        squares = jnp.zeros((rows, LANES), jnp.float32)
    for n in range(count):
        for b in range(spans):
            chunk = order[n * spans + b]
            piece = pieces[n][b]
            store[chunk - base] = piece
            squares += take_chunk(piece, g_ref, plain, hid_ref, chunk, chunks)
    mean = jnp.sum(squares, axis=-1, keepdims=True) * (1.0 / width)
    scaling = lax.rsqrt(mean + EPS)
    y = jnp.concatenate([store[j] for j in range(own)], axis=1)
    activated = []
    for n in range(HID // CHUNK):
        halves = []
        for start in (0, HID):
            cols = slice(start + n * CHUNK, start + (n + 1) * CHUNK)
            value = jnp.dot(y, gu_ref[:, cols], preferred_element_type=jnp.float32)
            if resumed:
                value = value + acc_ref[:, cols]
            halves.append(value * scaling)
        gate, up = halves
        activated.append((gate / (1.0 + jnp.exp(-gate)) * up).astype(jnp.bfloat16))
    activated = jnp.concatenate(activated, axis=1)
    mix = mix_ref[...]
    wide = width // 8
    for j in range(4):
        results = [
            jnp.dot(
                activated,
                dn_ref[0, :, start + j * wide : start + (j + 1) * wide],
                preferred_element_type=jnp.float32,
            )
            * mix
            for start in (0, width // 2)
        ]
        first[...] = jnp.where(side == 0, results[0], results[1])
        second[...] = jnp.where(side == 0, results[1], results[0])
        for n in range(outs):
            for b in range(blocks):
                span = pl.ds(pl.multiple_of(back[n * blocks + b] * 8, 8), 8)
                o_refs[n][b, :, j * wide : (j + 1) * wide] = jnp.concatenate(
                    [first[span, :], second[span, :]], axis=0
                ).astype(jnp.bfloat16)


def experts(pieces, gate_up, down_weight, norm_gain, mix, outs, begun=()):
    rows = mix.shape[0]
    width = down_weight.shape[2]
    chunks = width // CHUNK
    groups = rows // 8
    vmem_spec = pl.BlockSpec(memory_space=pltpu.VMEM)
    count = len(pieces)
    in_vmem = functools.partial(pltpu.with_memory_space_constraint, memory_space=pltpu.VMEM)
    return pl.pallas_call(
        functools.partial(expert_kernel, count, outs, bool(begun)),
        in_specs=[vmem_spec] * (count + 4 + len(begun)),
        out_specs=[vmem_spec] * (outs + 1),
        out_shape=[jax.ShapeDtypeStruct((groups // outs, 16, width // 2), jnp.bfloat16)] * outs
        + [jax.ShapeDtypeStruct((16, width // 2), jnp.float32)],
        scratch_shapes=[
            pltpu.VMEM((chunks // (2 if begun else 1), rows, CHUNK), jnp.bfloat16),
            pltpu.VMEM((rows, CHUNK), jnp.float32),
            pltpu.VMEM((rows, width // 8), jnp.float32),
            pltpu.VMEM((rows, width // 8), jnp.float32),
        ],
        compiler_params=pltpu.CompilerParams(vmem_limit_bytes=(8 if rows <= 128 else 24) * MIB),
        name="experts",
    )(
        *pieces,
        in_vmem(gate_up),
        in_vmem(down_weight),
        norm_gain.reshape(chunks, 1, CHUNK),
        mix,
        *begun,
    )


def body(
    query_heads,
    key_cache,
    value_cache,
    cache_lengths,
    out_weight,
    residual,
    norm_gain,
    expert_ids,
    route_weights,
    gate_up,
    down_weight,
):
    side = lax.axis_index("side")
    groups = lax.axis_size("grp")
    sessions, width = residual.shape
    half = sessions // 2
    rows = groups * half
    columns = width // groups
    arrays = (
        query_heads,
        key_cache,
        value_cache,
        cache_lengths,
        expert_ids,
        route_weights,
        norm_gain,
        residual,
    )
    if groups == CHIPS:
        *carried, gain = attend(groups, PLANES, *arrays)
        pieces = gather(carried)
        staged, done = stage(gate_up, pieces[11])
        y, mix = project([p[None] for p in pieces], out_weight, gain, waits=(done,))
        nears, fars = gather_pairs(y)
        begun = near(nears, staged, norm_gain)
        *sums, hidden = experts(fars, staged, down_weight, norm_gain, mix, 8, begun)
        mixture = scatter_sum(sums[:4], sums[4:])
    else:
        own_residual = lax.dynamic_slice_in_dim(residual, side * half, half, axis=0)
        residual_columns = lax.all_to_all(
            own_residual.reshape(half, groups, columns).transpose(1, 0, 2),
            "grp",
            split_axis=0,
            concat_axis=0,
            tiled=True,
        ).reshape(rows, columns)
        attn_out, gain = attend(groups, 0, *arrays)
        pieces = lax.all_gather(attn_out, "grp", axis=0)
        y, mix = project([pieces], out_weight, gain, residual_columns)
        y_all = lax.all_gather(y, "grp", axis=0).transpose(1, 0, 2)
        y_chunks = y_all.reshape(rows, width // CHUNK, CHUNK).transpose(1, 0, 2)
        *sums, hidden = experts([y_chunks], gate_up[0], down_weight, norm_gain, mix, 1)
        sent = lax.all_to_all(sums[0], "grp", split_axis=0, concat_axis=0, tiled=True)
        mixture = jnp.sum(sent.astype(jnp.float32), axis=0)
    ready = (hidden + mixture).astype(jnp.bfloat16)
    mine, other = ready[:half], ready[half:]
    other = lax.ppermute(other, "side", [(0, 1), (1, 0)])
    return jnp.where(
        side == 0, jnp.concatenate([mine, other]), jnp.concatenate([other, mine])
    )


def solution(mesh):
    return jax.shard_map(
        body,
        mesh=mesh,
        in_specs=(
            P("grp", None),
            P("grp", None, None),
            P("grp", None, None),
            P("grp"),
            P(None, "grp"),
            P("grp", None),
            P(),
            P("grp", None),
            P("grp", None),
            P("grp", None, None),
            P("grp", None, None),
        ),
        out_specs=P("grp", "side"),
        check_vma=False,
    )
```

```python
import functools

import jax
import jax.numpy as jnp
from jax import lax
from jax.experimental import pallas as pl
from jax.experimental.pallas import tpu as pltpu
from jax.sharding import PartitionSpec as P

HQ = 64
KVH = 4
HD = 128
HID = 768
TOPK = 8
CTX = 128
GROUP = HQ // KVH
EPS = 1e-06
CHUNK = 256
LANES = 128
MIB = 1 << 20


CHIPS = 16
PLANES = 4
PAIRS = ((0, 1), (2, 3))
BACK_PAIRS = ((2, 3), (0, 1))
ROUTING = LANES


def exchange(value, bits):
    return lax.ppermute(value, "grp", [(g, g ^ bits) for g in range(CHIPS)])


def piece_order(place, groups):
    if groups != CHIPS:
        return list(range(groups))
    return [place ^ n for n in range(CHIPS)]


def pair_order(place, groups, pairs):
    if groups != CHIPS:
        return list(range(groups))
    return [place ^ (4 * k + f) for pair in pairs for f in range(4) for k in pair]


def after(value, *done):
    return lax.optimization_barrier((value, *done))[0]


def gather(planes):
    own = planes[0]
    z1 = exchange(planes[1], 4)
    z2 = exchange(planes[2], 8)
    x0 = exchange(own, 1)
    y0 = exchange(own, 2)
    z3 = exchange(after(planes[3], z2), 12)
    c0 = exchange(x0, 2)
    x1 = exchange(after(x0, z1), 4)
    y1 = exchange(after(z1, z3), 2)
    x2 = exchange(after(z2, y0), 1)
    y2 = exchange(z2, 2)
    c1 = exchange(c0, 4)
    c2 = exchange(after(x2, x1, z2, z3), 2)
    x3 = exchange(after(z3, y2, x2), 1)
    y3 = exchange(z3, 2)
    c3 = exchange(after(y3, x1), 1)
    return [own, x0, y0, c0, z1, x1, y1, c1, z2, x2, y2, c2, z3, x3, y3, c3]


BY_NEXT_PLANE = (5, 7)


def gather_pairs(piece):
    column = [piece] + [exchange(piece, 4 * k) for k in range(1, PLANES)]
    near, far = (jnp.stack([column[k] for k in pair]) for pair in PAIRS)
    far = after(far, near)
    nears = [exchange(near, f) if f else near for f in range(4)]
    fars = [exchange(far, f) if f else far for f in range(4)]
    return nears, fars


def add(*terms):
    return sum(t.astype(jnp.float32) for t in terms).astype(jnp.bfloat16)


def scatter_sum(far, near):
    far = add(far[0], *[exchange(far[f], f) for f in (3, 1, 2)])
    near = add(near[0], *[exchange(near[f], f) for f in (3, 1, 2)])
    late = exchange(far[0], 8).astype(jnp.float32) + exchange(far[1], 12).astype(jnp.float32)
    late = lax.optimization_barrier(late)
    return near[0].astype(jnp.float32) + exchange(near[1], 4).astype(jnp.float32) + late


def attend_kernel(
    planes, ids_hbm, route_hbm, len_hbm, g_hbm, r_hbm, q_hbm, k_hbm, v_hbm, *refs
):
    o_refs = refs[: max(1, planes)]
    gain_ref = refs[max(1, planes)]
    o_ref = o_refs[0]
    len_ref, ids_ref, route_ref, tail_ref, r_ref, q_ref, k_ref, v_ref, sems = refs[-9:]
    side = lax.axis_index("side")
    half = k_ref.shape[0]
    rows = GROUP * half
    depth = HQ * HD // 2
    mine = [side * half + s for s in range(half)]
    small = [
        pltpu.make_async_copy(ids_hbm, ids_ref, sems.at[2 * half + 3]),
        pltpu.make_async_copy(route_hbm, route_ref, sems.at[2 * half + 4]),
    ]
    copies = [
        pltpu.make_async_copy(len_hbm, len_ref, sems.at[2 * half + 1]),
        pltpu.make_async_copy(q_hbm, q_ref, sems.at[2 * half]),
    ]
    copies += [
        pltpu.make_async_copy(k_hbm.at[mine[s]], k_ref.at[s], sems.at[s]) for s in range(half)
    ]
    late = [
        pltpu.make_async_copy(v_hbm.at[mine[s]], v_ref.at[s], sems.at[half + s])
        for s in range(half)
    ]
    late.append(pltpu.make_async_copy(r_hbm, r_ref, sems.at[2 * half + 2]))
    gain = g_hbm.at[lax.axis_index("grp")]
    late.append(pltpu.make_async_copy(gain, gain_ref, sems.at[2 * half + 5]))
    for copy in small + copies + late:
        copy.start()
    session = lax.broadcasted_iota(jnp.int32, (rows, CTX), 0) % half
    place = lax.broadcasted_iota(jnp.int32, (rows, CTX), 1)
    for copy in small:
        copy.wait()
    terms, rest = [], route_ref[...]
    for _ in range(3):
        terms.append(rest.astype(jnp.bfloat16).astype(jnp.float32))
        rest = rest - terms[-1]
    count = 2 * half
    tail_ref[...] = jnp.zeros_like(tail_ref)
    tail_ref[:, :count] = jnp.concatenate(terms[1:], axis=0)
    second = pltpu.roll(tail_ref[...], LANES // 2, axis=1)
    tail_ref[:, :count] = jnp.concatenate([ids_ref[...].astype(jnp.float32), terms[0]], axis=0)
    tail = jnp.where(
        lax.broadcasted_iota(jnp.int32, second.shape, 1) < LANES // 2, tail_ref[...], second
    ).astype(jnp.bfloat16)
    for ref in o_refs:
        ref[:, depth : depth + ROUTING] = tail

    for copy in copies:
        copy.wait()
    lives = [(session == s) & (place < len_ref[mine[s]]) for s in range(half)]
    spreads = []
    for kv in range(KVH):
        parts = []
        for h in range(kv * GROUP, (kv + 1) * GROUP):
            both = q_ref[:, h * HD : (h + 1) * HD].astype(jnp.float32)
            parts.append(jnp.where(side == 0, both[:half], both[half:]))
        queries = jnp.concatenate(parts, axis=0).astype(jnp.bfloat16)
        keys = k_ref[:, :, kv * HD : (kv + 1) * HD].reshape(half * CTX, HD)
        every = lax.dot_general(
            queries, keys, (((1,), (1,)), ((), ())), preferred_element_type=jnp.float32
        )
        scores = jnp.full((rows, CTX), -1e30, jnp.float32)
        for s in range(half):
            part = every[:, s * CTX : (s + 1) * CTX] * HD ** (-0.5)
            scores = jnp.where(lives[s], part, scores)
        lifted = jnp.exp(scores - jnp.max(scores, axis=-1, keepdims=True))
        weights = lifted / jnp.sum(lifted, axis=-1, keepdims=True)
        spreads.append(
            jnp.concatenate(
                [jnp.where(session == s, weights, 0.0).astype(jnp.bfloat16) for s in range(half)],
                axis=1,
            )
        )
    for copy in late:
        copy.wait()
    outs = []
    for kv in range(KVH):
        values = v_ref[:, :, kv * HD : (kv + 1) * HD].reshape(half * CTX, HD)
        outs.append(jnp.dot(spreads[kv], values, preferred_element_type=jnp.float32))
    later = KVH // 2
    for kv in range(later):
        for h in range(GROUP):
            pair = [out[h * half : (h + 1) * half] for out in (outs[kv], outs[kv + later])]
            both = jnp.concatenate(pair, axis=0).astype(jnp.bfloat16)
            for ref in o_refs:
                ref[:, (kv * GROUP + h) * HD : (kv * GROUP + h + 1) * HD] = both
    here = lax.axis_index("grp") // 4
    for k in range(planes):
        wide = r_ref.shape[1] // planes // 2
        parts = []
        for part in range(2):
            start = pl.multiple_of(((here ^ k) * 2 + part) * wide, wide)
            both = r_ref[:, pl.ds(start, wide)].astype(jnp.float32)
            parts.append(jnp.where(side == 0, both[:half], both[half:]))
        tail = jnp.concatenate(parts, axis=0).astype(jnp.bfloat16)
        o_refs[k][:, depth + ROUTING : depth + ROUTING + wide] = tail
        if k == 1:
            o_ref[:, depth + ROUTING + wide :] = tail


def attend(
    groups,
    planes,
    query_heads,
    key_cache,
    value_cache,
    cache_lengths,
    expert_ids,
    route_weights,
    norm_gain,
    residual,
):
    sessions, width = residual.shape
    half = sessions // 2
    columns = width // groups
    hbm_spec = pl.BlockSpec(memory_space=pltpu.HBM)
    vmem_spec = pl.BlockSpec(memory_space=pltpu.VMEM)
    in_hbm = functools.partial(pltpu.with_memory_space_constraint, memory_space=pltpu.HBM)
    outs = max(1, planes)
    tail = width // planes // 2 if planes else 0
    carried = [HQ * HD // 2 + ROUTING + tail * (2 if k == 0 else 1) for k in range(outs)]
    return pl.pallas_call(
        functools.partial(attend_kernel, planes),
        in_specs=[hbm_spec] * 8,
        out_specs=[vmem_spec] * (outs + 1),
        out_shape=[jax.ShapeDtypeStruct((sessions, n), jnp.bfloat16) for n in carried]
        + [jax.ShapeDtypeStruct((1, columns), jnp.float32)],
        scratch_shapes=[
            pltpu.SMEM((sessions,), jnp.int32),
            pltpu.VMEM((TOPK, sessions), jnp.int32),
            pltpu.VMEM((TOPK, sessions), jnp.float32),
            pltpu.VMEM((sessions, ROUTING), jnp.float32),
            pltpu.VMEM((sessions, width), jnp.bfloat16),
            pltpu.VMEM((sessions, HQ * HD), jnp.bfloat16),
            pltpu.VMEM((half, CTX, KVH * HD), jnp.bfloat16),
            pltpu.VMEM((half, CTX, KVH * HD), jnp.bfloat16),
            pltpu.SemaphoreType.DMA((2 * half + 6,)),
        ],
        compiler_params=pltpu.CompilerParams(vmem_limit_bytes=8 * MIB),
        name="attend",
    )(
        in_hbm(expert_ids.T),
        in_hbm(route_weights.T),
        in_hbm(cache_lengths),
        in_hbm(norm_gain.reshape(groups, 1, columns)),
        in_hbm(residual),
        in_hbm(query_heads),
        in_hbm(key_cache),
        in_hbm(value_cache),
    )


def project_kernel(count, waits, *refs):
    refs = refs[waits:]
    pieces = refs[:count]
    *rest, w_ref, g_ref, y_ref, mix_ref, plain = refs[count:]
    blocks, sessions, _ = pieces[0].shape
    depth = w_ref.shape[0] // 2
    half = sessions // 2
    columns = w_ref.shape[1]
    groups = count * blocks
    side, place = lax.axis_index("side"), lax.axis_index("grp")
    order = piece_order(place, groups)
    total = None
    for part in range(2):
        chunk = depth // 4
        for j in range(4):
            a = jnp.concatenate(
                [
                    piece[:, :, j * chunk : (j + 1) * chunk].reshape(blocks * sessions, chunk)
                    for piece in pieces
                ],
                axis=0,
            )
            start = part * depth + j * chunk
            term = jnp.dot(a, w_ref[start : start + chunk], preferred_element_type=jnp.float32)
            got = term if j == 0 else got + term
        got = got.reshape(groups, 2, half, columns)[:, part]
        total = got if total is None else total + got
    own = lax.broadcasted_iota(jnp.int32, (half, LANES), 1) == side * half + (
        lax.broadcasted_iota(jnp.int32, (half, LANES), 0)
    )
    for n in range(count):
        for b in range(blocks):
            span = pl.ds(pl.multiple_of(order[n * blocks + b] * half, half), half)
            value = total[n * blocks + b]
            if not rest:
                start = depth + ROUTING + (2 * columns if n in BY_NEXT_PLANE else 0)
                tail = pieces[n][b, :, start : start + 2 * columns].astype(jnp.float32)
                spot = place % 4
                tail = jnp.where(spot // 2 == 0, tail[:half], tail[half:])
                value = value + jnp.where(spot % 2 == 0, tail[:, :columns], tail[:, columns:])
            plain[span, :] = value
            first = pieces[n][b, :, depth : depth + ROUTING].astype(jnp.float32)
            second = pltpu.roll(first, LANES // 2, axis=1)
            weights = first[half:] + (second[:half] + second[half:])
            chosen = jnp.where(first[:half] == place.astype(jnp.float32), weights, 0.0)
            chosen = jnp.sum(chosen, axis=0, keepdims=True)
            mix_ref[span, :] = jnp.sum(jnp.where(own, chosen, 0.0), axis=1, keepdims=True)
    hidden = plain[...]
    if rest:
        hidden = hidden + rest[0][...].astype(jnp.float32)
    y_ref[...] = (hidden * g_ref[...]).astype(jnp.bfloat16)


def project(pieces, out_weight, gain_columns, residual_columns=None, waits=()):
    count = len(pieces)
    columns = out_weight.shape[1]
    rows = sum(p.shape[0] for p in pieces) * pieces[0].shape[1] // 2
    rest = [] if residual_columns is None else [residual_columns]
    vmem_spec = pl.BlockSpec(memory_space=pltpu.VMEM)
    return pl.pallas_call(
        functools.partial(project_kernel, count, len(waits)),
        in_specs=[pl.BlockSpec(memory_space=pl.ANY)] * len(waits)
        + [vmem_spec] * (count + len(rest) + 2),
        out_specs=[vmem_spec] * 2,
        out_shape=[
            jax.ShapeDtypeStruct((rows, columns), jnp.bfloat16),
            jax.ShapeDtypeStruct((rows, 1), jnp.float32),
        ],
        scratch_shapes=[pltpu.VMEM((rows, columns), jnp.float32)],
        compiler_params=pltpu.CompilerParams(vmem_limit_bytes=8 * MIB),
        name="project",
    )(
        *waits,
        *pieces,
        *rest,
        pltpu.with_memory_space_constraint(out_weight, pltpu.VMEM),
        gain_columns,
    )


def take_chunk(store, g_ref, plain, hid_ref, chunk, chunks):
    side, place = lax.axis_index("side"), lax.axis_index("grp")
    value = store.astype(jnp.float32) * (1.0 / g_ref[chunk])
    plain[...] = value
    local, late = chunk % (chunks // 2), chunk // (chunks // 2)
    rows = pl.ds(pl.multiple_of(8 * ((side + late) % 2), 8), 8)
    columns = pl.ds(pl.multiple_of(local * CHUNK, CHUNK), CHUNK)
    hid_ref[rows, columns] = plain[pl.ds(pl.multiple_of(place * 8, 8), 8), :]
    squares = value * value
    return squares[:, :LANES] + squares[:, LANES:]


def stage_kernel(_, gu_hbm, weights, done, sems):
    copies = [
        pltpu.make_async_copy(
            gu_hbm.at[0, pl.ds(j * CHUNK, CHUNK)], weights.at[pl.ds(j * CHUNK, CHUNK)], sems.at[j]
        )
        for j in range(weights.shape[0] // CHUNK)
    ]
    for copy in copies:
        copy.start()
    done[...] = jnp.zeros_like(done)
    for copy in copies:
        copy.wait()


def stage(gate_up, arrived):
    depth = gate_up.shape[1]
    hbm_spec = pl.BlockSpec(memory_space=pltpu.HBM)
    vmem_spec = pl.BlockSpec(memory_space=pltpu.VMEM)
    return pl.pallas_call(
        stage_kernel,
        in_specs=[pl.BlockSpec(memory_space=pl.ANY), hbm_spec],
        out_specs=[vmem_spec] * 2,
        out_shape=[
            jax.ShapeDtypeStruct((depth, 2 * HID), jnp.bfloat16),
            jax.ShapeDtypeStruct((8, LANES), jnp.float32),
        ],
        scratch_shapes=[pltpu.SemaphoreType.DMA((depth // CHUNK,))],
        compiler_params=pltpu.CompilerParams(vmem_limit_bytes=2 * MIB),
        cost_estimate=pl.CostEstimate(
            flops=0, bytes_accessed=depth * 4 * HID, transcendentals=0
        ),
        name="stage",
    )(arrived, pltpu.with_memory_space_constraint(gate_up, pltpu.HBM))


def near_kernel(count, *refs):
    pieces = refs[:count]
    weights, g_ref, acc, sq_ref, hid_ref, store, plain = refs[count:]
    place = lax.axis_index("grp")
    chunks = g_ref.shape[0]
    own = chunks // 2
    first = (place // (CHIPS // 2)) * own
    order = pair_order(place, CHIPS, PAIRS)[:own]
    mine = weights.at[pl.ds(pl.multiple_of(first * CHUNK, CHUNK), own * CHUNK)]
    squares = jnp.zeros(sq_ref.shape, jnp.float32)
    for n in range(count):
        for b in range(2):
            chunk = order[2 * n + b]
            piece = pieces[n][b]
            store[chunk - first] = piece
            squares += take_chunk(piece, g_ref, plain, hid_ref, chunk, chunks)
    sq_ref[...] = squares
    y = jnp.concatenate([store[j] for j in range(own)], axis=1)
    for n in range(2 * HID // CHUNK):
        cols = slice(n * CHUNK, (n + 1) * CHUNK)
        acc[:, cols] = jnp.dot(y, mine[:, cols], preferred_element_type=jnp.float32)


def near(pieces, staged, norm_gain):
    rows = pieces[0].shape[1]
    width = staged.shape[0]
    chunks = width // CHUNK
    vmem_spec = pl.BlockSpec(memory_space=pltpu.VMEM)
    count = len(pieces)
    return pl.pallas_call(
        functools.partial(near_kernel, count),
        in_specs=[vmem_spec] * (count + 2),
        out_specs=[vmem_spec] * 3,
        out_shape=[
            jax.ShapeDtypeStruct((rows, 2 * HID), jnp.float32),
            jax.ShapeDtypeStruct((rows, LANES), jnp.float32),
            jax.ShapeDtypeStruct((16, width // 2), jnp.float32),
        ],
        scratch_shapes=[
            pltpu.VMEM((chunks // 2, rows, CHUNK), jnp.bfloat16),
            pltpu.VMEM((rows, CHUNK), jnp.float32),
        ],
        compiler_params=pltpu.CompilerParams(vmem_limit_bytes=6 * MIB),
        cost_estimate=pl.CostEstimate(
            flops=2 * rows * width * HID, bytes_accessed=width * 4 * HID, transcendentals=0
        ),
        name="near",
    )(
        *pieces,
        pltpu.with_memory_space_constraint(staged, pltpu.VMEM),
        norm_gain.reshape(chunks, 1, CHUNK),
    )


def expert_kernel(count, outs, resumed, *refs):
    pieces = refs[:count]
    gu_ref, dn_ref, g_ref, mix_ref = refs[count : count + 4]
    rest = refs[count + 4 :]
    if resumed:
        acc_ref, sq_ref, old_ref = rest[:3]
        rest = rest[3:]
    o_refs, (hid_ref, store, plain, first, second) = rest[:outs], rest[outs:]
    side, place = lax.axis_index("side"), lax.axis_index("grp")
    own, rows, _ = store.shape
    chunks = g_ref.shape[0]
    width = chunks * CHUNK
    groups = rows // 8
    blocks = groups // outs
    spans = pieces[0].shape[0]
    back = pair_order(place, groups, BACK_PAIRS)
    if resumed:
        order = pair_order(place, groups, PAIRS)[own:]
        base = own - (place // (CHIPS // 2)) * own
        gu_ref = gu_ref.at[pl.ds(pl.multiple_of(base * CHUNK, CHUNK), own * CHUNK)]
        squares = sq_ref[...]
        hid_ref[...] = old_ref[...]
    else:
        order, base = list(range(chunks)), 0
        squares = jnp.zeros((rows, LANES), jnp.float32)
    for n in range(count):
        for b in range(spans):
            chunk = order[n * spans + b]
            piece = pieces[n][b]
            store[chunk - base] = piece
            squares += take_chunk(piece, g_ref, plain, hid_ref, chunk, chunks)
    mean = jnp.sum(squares, axis=-1, keepdims=True) * (1.0 / width)
    scaling = lax.rsqrt(mean + EPS)
    y = jnp.concatenate([store[j] for j in range(own)], axis=1)
    activated = []
    for n in range(HID // CHUNK):
        halves = []
        for start in (0, HID):
            cols = slice(start + n * CHUNK, start + (n + 1) * CHUNK)
            value = jnp.dot(y, gu_ref[:, cols], preferred_element_type=jnp.float32)
            if resumed:
                value = value + acc_ref[:, cols]
            halves.append(value * scaling)
        gate, up = halves
        activated.append((gate / (1.0 + jnp.exp(-gate)) * up).astype(jnp.bfloat16))
    activated = jnp.concatenate(activated, axis=1)
    mix = mix_ref[...]
    wide = width // 8
    for j in range(4):
        results = [
            jnp.dot(
                activated,
                dn_ref[0, :, start + j * wide : start + (j + 1) * wide],
                preferred_element_type=jnp.float32,
            )
            * mix
            for start in (0, width // 2)
        ]
        first[...] = jnp.where(side == 0, results[0], results[1])
        second[...] = jnp.where(side == 0, results[1], results[0])
        for n in range(outs):
            for b in range(blocks):
                span = pl.ds(pl.multiple_of(back[n * blocks + b] * 8, 8), 8)
                o_refs[n][b, :, j * wide : (j + 1) * wide] = jnp.concatenate(
                    [first[span, :], second[span, :]], axis=0
                ).astype(jnp.bfloat16)


def experts(pieces, gate_up, down_weight, norm_gain, mix, outs, begun=()):
    rows = mix.shape[0]
    width = down_weight.shape[2]
    chunks = width // CHUNK
    groups = rows // 8
    vmem_spec = pl.BlockSpec(memory_space=pltpu.VMEM)
    count = len(pieces)
    in_vmem = functools.partial(pltpu.with_memory_space_constraint, memory_space=pltpu.VMEM)
    return pl.pallas_call(
        functools.partial(expert_kernel, count, outs, bool(begun)),
        in_specs=[vmem_spec] * (count + 4 + len(begun)),
        out_specs=[vmem_spec] * (outs + 1),
        out_shape=[jax.ShapeDtypeStruct((groups // outs, 16, width // 2), jnp.bfloat16)] * outs
        + [jax.ShapeDtypeStruct((16, width // 2), jnp.float32)],
        scratch_shapes=[
            pltpu.VMEM((chunks // (2 if begun else 1), rows, CHUNK), jnp.bfloat16),
            pltpu.VMEM((rows, CHUNK), jnp.float32),
            pltpu.VMEM((rows, width // 8), jnp.float32),
            pltpu.VMEM((rows, width // 8), jnp.float32),
        ],
        compiler_params=pltpu.CompilerParams(vmem_limit_bytes=(8 if rows <= 128 else 24) * MIB),
        name="experts",
    )(
        *pieces,
        in_vmem(gate_up),
        in_vmem(down_weight),
        norm_gain.reshape(chunks, 1, CHUNK),
        mix,
        *begun,
    )


def body(
    query_heads,
    key_cache,
    value_cache,
    cache_lengths,
    out_weight,
    residual,
    norm_gain,
    expert_ids,
    route_weights,
    gate_up,
    down_weight,
):
    side = lax.axis_index("side")
    groups = lax.axis_size("grp")
    sessions, width = residual.shape
    half = sessions // 2
    rows = groups * half
    columns = width // groups
    arrays = (
        query_heads,
        key_cache,
        value_cache,
        cache_lengths,
        expert_ids,
        route_weights,
        norm_gain,
        residual,
    )
    if groups == CHIPS:
        *carried, gain = attend(groups, PLANES, *arrays)
        pieces = gather(carried)
        staged, done = stage(gate_up, pieces[9])
        y, mix = project([p[None] for p in pieces], out_weight, gain, waits=(done,))
        nears, fars = gather_pairs(y)
        begun = near(nears, staged, norm_gain)
        *sums, hidden = experts(fars, staged, down_weight, norm_gain, mix, 8, begun)
        mixture = scatter_sum(sums[:4], sums[4:])
    else:
        own_residual = lax.dynamic_slice_in_dim(residual, side * half, half, axis=0)
        residual_columns = lax.all_to_all(
            own_residual.reshape(half, groups, columns).transpose(1, 0, 2),
            "grp",
            split_axis=0,
            concat_axis=0,
            tiled=True,
        ).reshape(rows, columns)
        attn_out, gain = attend(groups, 0, *arrays)
        pieces = lax.all_gather(attn_out, "grp", axis=0)
        y, mix = project([pieces], out_weight, gain, residual_columns)
        y_all = lax.all_gather(y, "grp", axis=0).transpose(1, 0, 2)
        y_chunks = y_all.reshape(rows, width // CHUNK, CHUNK).transpose(1, 0, 2)
        *sums, hidden = experts([y_chunks], gate_up[0], down_weight, norm_gain, mix, 1)
        sent = lax.all_to_all(sums[0], "grp", split_axis=0, concat_axis=0, tiled=True)
        mixture = jnp.sum(sent.astype(jnp.float32), axis=0)
    ready = (hidden + mixture).astype(jnp.bfloat16)
    mine, other = ready[:half], ready[half:]
    other = lax.ppermute(other, "side", [(0, 1), (1, 0)])
    return jnp.where(
        side == 0, jnp.concatenate([mine, other]), jnp.concatenate([other, mine])
    )


def solution(mesh):
    return jax.shard_map(
        body,
        mesh=mesh,
        in_specs=(
            P("grp", None),
            P("grp", None, None),
            P("grp", None, None),
            P("grp"),
            P(None, "grp"),
            P("grp", None),
            P(),
            P("grp", None),
            P("grp", None),
            P("grp", None, None),
            P("grp", None, None),
        ),
        out_specs=P("grp", "side"),
        check_vma=False,
    )
```

```python
import functools

import jax
import jax.numpy as jnp
from jax import lax
from jax.experimental import pallas as pl
from jax.experimental.pallas import tpu as pltpu
from jax.sharding import PartitionSpec as P

HQ = 64
KVH = 4
HD = 128
HID = 768
TOPK = 8
CTX = 128
GROUP = HQ // KVH
EPS = 1e-06
CHUNK = 256
LANES = 128
MIB = 1 << 20


CHIPS = 16
PLANES = 4
PAIRS = ((0, 1), (2, 3))
BACK_PAIRS = ((2, 3), (0, 1))
ROUTING = LANES


def exchange(value, bits):
    return lax.ppermute(value, "grp", [(g, g ^ bits) for g in range(CHIPS)])


def piece_order(place, groups):
    if groups != CHIPS:
        return list(range(groups))
    return [place ^ n for n in range(CHIPS)]


def pair_order(place, groups, pairs):
    if groups != CHIPS:
        return list(range(groups))
    return [place ^ (4 * k + f) for pair in pairs for f in range(4) for k in pair]


def after(value, *done):
    return lax.optimization_barrier((value, *done))[0]


def gather(planes):
    own = planes[0]
    z1 = exchange(planes[1], 4)
    z2 = exchange(planes[2], 8)
    x0 = exchange(own, 1)
    y0 = exchange(own, 2)
    z3 = exchange(after(planes[3], z2), 12)
    c0 = exchange(x0, 2)
    x1 = exchange(after(x0, z1), 4)
    y1 = exchange(after(z1, z3), 2)
    x2 = exchange(after(z2, y0), 1)
    y2 = exchange(z2, 2)
    c1 = exchange(c0, 4)
    c2 = exchange(after(x2, x1, z2, z3), 2)
    x3 = exchange(after(z3, y2, x2), 1)
    y3 = exchange(z3, 2)
    c3 = exchange(after(y3, x1), 1)
    return [own, x0, y0, c0, z1, x1, y1, c1, z2, x2, y2, c2, z3, x3, y3, c3]


BY_NEXT_PLANE = (5, 7)


def gather_pairs(piece):
    column = [piece] + [exchange(piece, 4 * k) for k in range(1, PLANES)]
    near, far = (jnp.stack([column[k] for k in pair]) for pair in PAIRS)
    far = after(far, near)
    nears = [exchange(near, f) if f else near for f in range(4)]
    fars = [exchange(far, f) if f else far for f in range(4)]
    return nears, fars


def add(*terms):
    return sum(t.astype(jnp.float32) for t in terms).astype(jnp.bfloat16)


def scatter_sum(far, near):
    far = add(far[0], *[exchange(far[f], f) for f in (3, 1, 2)])
    near = add(near[0], *[exchange(near[f], f) for f in (3, 1, 2)])
    late = exchange(far[0], 8).astype(jnp.float32) + exchange(far[1], 12).astype(jnp.float32)
    late = lax.optimization_barrier(late)
    return near[0].astype(jnp.float32) + exchange(near[1], 4).astype(jnp.float32) + late


def attend_kernel(
    planes, ids_hbm, route_hbm, len_hbm, g_hbm, r_hbm, q_hbm, k_hbm, v_hbm, *refs
):
    o_refs = refs[: max(1, planes)]
    gain_ref = refs[max(1, planes)]
    o_ref = o_refs[0]
    len_ref, ids_ref, route_ref, tail_ref, r_ref, q_ref, k_ref, v_ref, sems = refs[-9:]
    side = lax.axis_index("side")
    half = k_ref.shape[0]
    rows = GROUP * half
    depth = HQ * HD // 2
    mine = [side * half + s for s in range(half)]
    small = [
        pltpu.make_async_copy(ids_hbm, ids_ref, sems.at[2 * half + 3]),
        pltpu.make_async_copy(route_hbm, route_ref, sems.at[2 * half + 4]),
    ]
    copies = [
        pltpu.make_async_copy(len_hbm, len_ref, sems.at[2 * half + 1]),
        pltpu.make_async_copy(q_hbm, q_ref, sems.at[2 * half]),
    ]
    copies += [
        pltpu.make_async_copy(k_hbm.at[mine[s]], k_ref.at[s], sems.at[s]) for s in range(half)
    ]
    late = [
        pltpu.make_async_copy(v_hbm.at[mine[s]], v_ref.at[s], sems.at[half + s])
        for s in range(half)
    ]
    late.append(pltpu.make_async_copy(r_hbm, r_ref, sems.at[2 * half + 2]))
    gain = g_hbm.at[lax.axis_index("grp")]
    late.append(pltpu.make_async_copy(gain, gain_ref, sems.at[2 * half + 5]))
    for copy in small + copies + late:
        copy.start()
    session = lax.broadcasted_iota(jnp.int32, (rows, CTX), 0) % half
    place = lax.broadcasted_iota(jnp.int32, (rows, CTX), 1)
    for copy in small:
        copy.wait()
    terms, rest = [], route_ref[...]
    for _ in range(3):
        terms.append(rest.astype(jnp.bfloat16).astype(jnp.float32))
        rest = rest - terms[-1]
    count = 2 * half
    tail_ref[...] = jnp.zeros_like(tail_ref)
    tail_ref[:, :count] = jnp.concatenate(terms[1:], axis=0)
    second = pltpu.roll(tail_ref[...], LANES // 2, axis=1)
    tail_ref[:, :count] = jnp.concatenate([ids_ref[...].astype(jnp.float32), terms[0]], axis=0)
    tail = jnp.where(
        lax.broadcasted_iota(jnp.int32, second.shape, 1) < LANES // 2, tail_ref[...], second
    ).astype(jnp.bfloat16)
    for ref in o_refs:
        ref[:, depth : depth + ROUTING] = tail

    for copy in copies:
        copy.wait()
    lives = [(session == s) & (place < len_ref[mine[s]]) for s in range(half)]
    spreads = []
    for kv in range(KVH):
        parts = []
        for h in range(kv * GROUP, (kv + 1) * GROUP):
            both = q_ref[:, h * HD : (h + 1) * HD].astype(jnp.float32)
            parts.append(jnp.where(side == 0, both[:half], both[half:]))
        queries = jnp.concatenate(parts, axis=0).astype(jnp.bfloat16)
        keys = k_ref[:, :, kv * HD : (kv + 1) * HD].reshape(half * CTX, HD)
        every = lax.dot_general(
            queries, keys, (((1,), (1,)), ((), ())), preferred_element_type=jnp.float32
        )
        scores = jnp.full((rows, CTX), -1e30, jnp.float32)
        for s in range(half):
            part = every[:, s * CTX : (s + 1) * CTX] * HD ** (-0.5)
            scores = jnp.where(lives[s], part, scores)
        lifted = jnp.exp(scores - jnp.max(scores, axis=-1, keepdims=True))
        weights = lifted / jnp.sum(lifted, axis=-1, keepdims=True)
        spreads.append(
            jnp.concatenate(
                [jnp.where(session == s, weights, 0.0).astype(jnp.bfloat16) for s in range(half)],
                axis=1,
            )
        )
    for copy in late:
        copy.wait()
    outs = []
    for kv in range(KVH):
        values = v_ref[:, :, kv * HD : (kv + 1) * HD].reshape(half * CTX, HD)
        outs.append(jnp.dot(spreads[kv], values, preferred_element_type=jnp.float32))
    later = KVH // 2
    for kv in range(later):
        for h in range(GROUP):
            pair = [out[h * half : (h + 1) * half] for out in (outs[kv], outs[kv + later])]
            both = jnp.concatenate(pair, axis=0).astype(jnp.bfloat16)
            for ref in o_refs:
                ref[:, (kv * GROUP + h) * HD : (kv * GROUP + h + 1) * HD] = both
    here = lax.axis_index("grp") // 4
    for k in range(planes):
        wide = r_ref.shape[1] // planes // 2
        parts = []
        for part in range(2):
            start = pl.multiple_of(((here ^ k) * 2 + part) * wide, wide)
            both = r_ref[:, pl.ds(start, wide)].astype(jnp.float32)
            parts.append(jnp.where(side == 0, both[:half], both[half:]))
        tail = jnp.concatenate(parts, axis=0).astype(jnp.bfloat16)
        o_refs[k][:, depth + ROUTING : depth + ROUTING + wide] = tail
        if k == 1:
            o_ref[:, depth + ROUTING + wide :] = tail


def attend(
    groups,
    planes,
    query_heads,
    key_cache,
    value_cache,
    cache_lengths,
    expert_ids,
    route_weights,
    norm_gain,
    residual,
):
    sessions, width = residual.shape
    half = sessions // 2
    columns = width // groups
    hbm_spec = pl.BlockSpec(memory_space=pltpu.HBM)
    vmem_spec = pl.BlockSpec(memory_space=pltpu.VMEM)
    in_hbm = functools.partial(pltpu.with_memory_space_constraint, memory_space=pltpu.HBM)
    outs = max(1, planes)
    tail = width // planes // 2 if planes else 0
    carried = [HQ * HD // 2 + ROUTING + tail * (2 if k == 0 else 1) for k in range(outs)]
    return pl.pallas_call(
        functools.partial(attend_kernel, planes),
        in_specs=[hbm_spec] * 8,
        out_specs=[vmem_spec] * (outs + 1),
        out_shape=[jax.ShapeDtypeStruct((sessions, n), jnp.bfloat16) for n in carried]
        + [jax.ShapeDtypeStruct((1, columns), jnp.float32)],
        scratch_shapes=[
            pltpu.SMEM((sessions,), jnp.int32),
            pltpu.VMEM((TOPK, sessions), jnp.int32),
            pltpu.VMEM((TOPK, sessions), jnp.float32),
            pltpu.VMEM((sessions, ROUTING), jnp.float32),
            pltpu.VMEM((sessions, width), jnp.bfloat16),
            pltpu.VMEM((sessions, HQ * HD), jnp.bfloat16),
            pltpu.VMEM((half, CTX, KVH * HD), jnp.bfloat16),
            pltpu.VMEM((half, CTX, KVH * HD), jnp.bfloat16),
            pltpu.SemaphoreType.DMA((2 * half + 6,)),
        ],
        compiler_params=pltpu.CompilerParams(vmem_limit_bytes=8 * MIB),
        name="attend",
    )(
        in_hbm(expert_ids.T),
        in_hbm(route_weights.T),
        in_hbm(cache_lengths),
        in_hbm(norm_gain.reshape(groups, 1, columns)),
        in_hbm(residual),
        in_hbm(query_heads),
        in_hbm(key_cache),
        in_hbm(value_cache),
    )


def project_kernel(count, staged, *refs):
    copies = []
    if staged:
        _, gu_hbm, *refs, quarter, plain, sems = refs
        refs.append(plain)
        chunks = gu_hbm.shape[1] // CHUNK
        copies = weight_copies(gu_hbm, quarter, sems, first_chunk(1, chunks))
    for copy in copies:
        copy.start()
    pieces = refs[:count]
    *rest, w_ref, g_ref, y_ref, mix_ref, plain = refs[count:]
    blocks, sessions, _ = pieces[0].shape
    depth = w_ref.shape[0] // 2
    half = sessions // 2
    columns = w_ref.shape[1]
    groups = count * blocks
    side, place = lax.axis_index("side"), lax.axis_index("grp")
    order = piece_order(place, groups)
    total = None
    for part in range(2):
        chunk = depth // 4
        for j in range(4):
            a = jnp.concatenate(
                [
                    piece[:, :, j * chunk : (j + 1) * chunk].reshape(blocks * sessions, chunk)
                    for piece in pieces
                ],
                axis=0,
            )
            start = part * depth + j * chunk
            term = jnp.dot(a, w_ref[start : start + chunk], preferred_element_type=jnp.float32)
            got = term if j == 0 else got + term
        got = got.reshape(groups, 2, half, columns)[:, part]
        total = got if total is None else total + got
    own = lax.broadcasted_iota(jnp.int32, (half, LANES), 1) == side * half + (
        lax.broadcasted_iota(jnp.int32, (half, LANES), 0)
    )
    for n in range(count):
        for b in range(blocks):
            span = pl.ds(pl.multiple_of(order[n * blocks + b] * half, half), half)
            value = total[n * blocks + b]
            if not rest:
                start = depth + ROUTING + (2 * columns if n in BY_NEXT_PLANE else 0)
                tail = pieces[n][b, :, start : start + 2 * columns].astype(jnp.float32)
                spot = place % 4
                tail = jnp.where(spot // 2 == 0, tail[:half], tail[half:])
                value = value + jnp.where(spot % 2 == 0, tail[:, :columns], tail[:, columns:])
            plain[span, :] = value
            first = pieces[n][b, :, depth : depth + ROUTING].astype(jnp.float32)
            second = pltpu.roll(first, LANES // 2, axis=1)
            weights = first[half:] + (second[:half] + second[half:])
            chosen = jnp.where(first[:half] == place.astype(jnp.float32), weights, 0.0)
            chosen = jnp.sum(chosen, axis=0, keepdims=True)
            mix_ref[span, :] = jnp.sum(jnp.where(own, chosen, 0.0), axis=1, keepdims=True)
    hidden = plain[...]
    if rest:
        hidden = hidden + rest[0][...].astype(jnp.float32)
    y_ref[...] = (hidden * g_ref[...]).astype(jnp.bfloat16)
    for copy in copies:
        copy.wait()


def project(pieces, out_weight, gain_columns, residual_columns=None, staged=()):
    count = len(pieces)
    columns = out_weight.shape[1]
    rows = sum(p.shape[0] for p in pieces) * pieces[0].shape[1] // 2
    rest = [] if residual_columns is None else [residual_columns]
    vmem_spec = pl.BlockSpec(memory_space=pltpu.VMEM)
    extra_specs, extra, extra_shapes, extra_scratch = [], [], [], []
    if staged:
        done, gate_up = staged
        quarter = gate_up.shape[1] // 4
        extra_specs = [pl.BlockSpec(memory_space=pl.ANY), pl.BlockSpec(memory_space=pltpu.HBM)]
        extra = [done, pltpu.with_memory_space_constraint(gate_up, pltpu.HBM)]
        extra_shapes = [jax.ShapeDtypeStruct((quarter, 2 * HID), jnp.bfloat16)]
        extra_scratch = [pltpu.SemaphoreType.DMA((quarter // CHUNK,))]
    return pl.pallas_call(
        functools.partial(project_kernel, count, bool(staged)),
        in_specs=extra_specs + [vmem_spec] * (count + len(rest) + 2),
        out_specs=[vmem_spec] * (2 + len(extra_shapes)),
        out_shape=[
            jax.ShapeDtypeStruct((rows, columns), jnp.bfloat16),
            jax.ShapeDtypeStruct((rows, 1), jnp.float32),
        ]
        + extra_shapes,
        scratch_shapes=[pltpu.VMEM((rows, columns), jnp.float32)] + extra_scratch,
        compiler_params=pltpu.CompilerParams(vmem_limit_bytes=8 * MIB),
        name="project",
    )(
        *extra,
        *pieces,
        *rest,
        pltpu.with_memory_space_constraint(out_weight, pltpu.VMEM),
        gain_columns,
    )


def take_chunk(store, g_ref, plain, hid_ref, chunk, chunks):
    side, place = lax.axis_index("side"), lax.axis_index("grp")
    value = store.astype(jnp.float32) * (1.0 / g_ref[chunk])
    plain[...] = value
    local, late = chunk % (chunks // 2), chunk // (chunks // 2)
    rows = pl.ds(pl.multiple_of(8 * ((side + late) % 2), 8), 8)
    columns = pl.ds(pl.multiple_of(local * CHUNK, CHUNK), CHUNK)
    hid_ref[rows, columns] = plain[pl.ds(pl.multiple_of(place * 8, 8), 8), :]
    squares = value * value
    return squares[:, :LANES] + squares[:, LANES:]


def weight_copies(gu_hbm, dst, sems, first):
    return [
        pltpu.make_async_copy(
            gu_hbm.at[0, pl.ds(pl.multiple_of((first + j) * CHUNK, CHUNK), CHUNK)],
            dst.at[pl.ds(j * CHUNK, CHUNK)],
            sems.at[j],
        )
        for j in range(dst.shape[0] // CHUNK)
    ]


def first_chunk(half, chunks):
    return ((lax.axis_index("grp") // (CHIPS // 2)) ^ half) * (chunks // 2)


def stage_kernel(_, gu_hbm, weights, done, sems):
    chunks = gu_hbm.shape[1] // CHUNK
    copies = weight_copies(gu_hbm, weights, sems, first_chunk(0, chunks))
    for copy in copies:
        copy.start()
    done[...] = jnp.zeros_like(done)
    for copy in copies:
        copy.wait()


def stage(gate_up, arrived):
    depth = gate_up.shape[1] // 2
    hbm_spec = pl.BlockSpec(memory_space=pltpu.HBM)
    vmem_spec = pl.BlockSpec(memory_space=pltpu.VMEM)
    return pl.pallas_call(
        stage_kernel,
        in_specs=[pl.BlockSpec(memory_space=pl.ANY), hbm_spec],
        out_specs=[vmem_spec] * 2,
        out_shape=[
            jax.ShapeDtypeStruct((depth, 2 * HID), jnp.bfloat16),
            jax.ShapeDtypeStruct((8, LANES), jnp.float32),
        ],
        scratch_shapes=[pltpu.SemaphoreType.DMA((depth // CHUNK,))],
        compiler_params=pltpu.CompilerParams(vmem_limit_bytes=2 * MIB),
        cost_estimate=pl.CostEstimate(
            flops=0, bytes_accessed=depth * 4 * HID, transcendentals=0
        ),
        name="stage",
    )(arrived, pltpu.with_memory_space_constraint(gate_up, pltpu.HBM))


def near_kernel(count, *refs):
    pieces = refs[:count]
    weights, gu_hbm, g_ref, acc, sq_ref, hid_ref, quarter, store, plain, sems = refs[count:]
    chunks = g_ref.shape[0]
    own = chunks // 2
    copies = weight_copies(gu_hbm, quarter, sems, first_chunk(1, chunks) + own // 2)
    for copy in copies:
        copy.start()
    order = pair_order(lax.axis_index("grp"), CHIPS, PAIRS)[:own]
    squares = jnp.zeros(sq_ref.shape, jnp.float32)
    for n in range(count):
        for b in range(2):
            chunk = order[2 * n + b]
            piece = pieces[n][b]
            store[chunk - first_chunk(0, chunks)] = piece
            squares += take_chunk(piece, g_ref, plain, hid_ref, chunk, chunks)
    sq_ref[...] = squares
    y = jnp.concatenate([store[j] for j in range(own)], axis=1)
    for n in range(2 * HID // CHUNK):
        cols = slice(n * CHUNK, (n + 1) * CHUNK)
        acc[:, cols] = jnp.dot(y, weights[:, cols], preferred_element_type=jnp.float32)
    for copy in copies:
        copy.wait()


def near(pieces, staged, gate_up, norm_gain):
    rows = pieces[0].shape[1]
    width = gate_up.shape[1]
    chunks = width // CHUNK
    vmem_spec = pl.BlockSpec(memory_space=pltpu.VMEM)
    count = len(pieces)
    return pl.pallas_call(
        functools.partial(near_kernel, count),
        in_specs=[vmem_spec] * (count + 1) + [pl.BlockSpec(memory_space=pltpu.HBM), vmem_spec],
        out_specs=[vmem_spec] * 4,
        out_shape=[
            jax.ShapeDtypeStruct((rows, 2 * HID), jnp.float32),
            jax.ShapeDtypeStruct((rows, LANES), jnp.float32),
            jax.ShapeDtypeStruct((16, width // 2), jnp.float32),
            jax.ShapeDtypeStruct((width // 4, 2 * HID), jnp.bfloat16),
        ],
        scratch_shapes=[
            pltpu.VMEM((chunks // 2, rows, CHUNK), jnp.bfloat16),
            pltpu.VMEM((rows, CHUNK), jnp.float32),
            pltpu.SemaphoreType.DMA((chunks // 4,)),
        ],
        compiler_params=pltpu.CompilerParams(vmem_limit_bytes=6 * MIB),
        cost_estimate=pl.CostEstimate(
            flops=2 * rows * width * HID, bytes_accessed=width * 4 * HID, transcendentals=0
        ),
        name="near",
    )(
        *pieces,
        pltpu.with_memory_space_constraint(staged, pltpu.VMEM),
        pltpu.with_memory_space_constraint(gate_up, pltpu.HBM),
        norm_gain.reshape(chunks, 1, CHUNK),
    )


def expert_kernel(count, outs, parts, resumed, *refs):
    pieces = refs[:count]
    gu_refs = refs[count : count + parts]
    dn_ref, g_ref, mix_ref, *rest = refs[count + parts :]
    if resumed:
        acc_ref, sq_ref, old_ref = rest[:3]
        rest = rest[3:]
    o_refs, (hid_ref, store, plain, first, second) = rest[:outs], rest[outs:]
    side, place = lax.axis_index("side"), lax.axis_index("grp")
    own, rows, _ = store.shape
    chunks = g_ref.shape[0]
    width = chunks * CHUNK
    groups = rows // 8
    blocks = groups // outs
    spans = pieces[0].shape[0]
    back = pair_order(place, groups, BACK_PAIRS)
    if resumed:
        order = pair_order(place, groups, PAIRS)[own:]
        base = first_chunk(1, chunks)
        squares = sq_ref[...]
        hid_ref[...] = old_ref[...]
    else:
        order, base = list(range(chunks)), 0
        squares = jnp.zeros((rows, LANES), jnp.float32)
    for n in range(count):
        for b in range(spans):
            chunk = order[n * spans + b]
            piece = pieces[n][b]
            store[chunk - base] = piece
            squares += take_chunk(piece, g_ref, plain, hid_ref, chunk, chunks)
    mean = jnp.sum(squares, axis=-1, keepdims=True) * (1.0 / width)
    scaling = lax.rsqrt(mean + EPS)
    span = own // parts
    ys = [
        jnp.concatenate([store[p * span + j] for j in range(span)], axis=1) for p in range(parts)
    ]
    activated = []
    for n in range(HID // CHUNK):
        halves = []
        for start in (0, HID):
            cols = slice(start + n * CHUNK, start + (n + 1) * CHUNK)
            value = sum(
                jnp.dot(y, gu_ref[:, cols], preferred_element_type=jnp.float32)
                for y, gu_ref in zip(ys, gu_refs)
            )
            if resumed:
                value = value + acc_ref[:, cols]
            halves.append(value * scaling)
        gate, up = halves
        activated.append((gate / (1.0 + jnp.exp(-gate)) * up).astype(jnp.bfloat16))
    activated = jnp.concatenate(activated, axis=1)
    mix = mix_ref[...]
    wide = width // 8
    for j in range(4):
        results = [
            jnp.dot(
                activated,
                dn_ref[0, :, start + j * wide : start + (j + 1) * wide],
                preferred_element_type=jnp.float32,
            )
            * mix
            for start in (0, width // 2)
        ]
        first[...] = jnp.where(side == 0, results[0], results[1])
        second[...] = jnp.where(side == 0, results[1], results[0])
        for n in range(outs):
            for b in range(blocks):
                span = pl.ds(pl.multiple_of(back[n * blocks + b] * 8, 8), 8)
                o_refs[n][b, :, j * wide : (j + 1) * wide] = jnp.concatenate(
                    [first[span, :], second[span, :]], axis=0
                ).astype(jnp.bfloat16)


def experts(pieces, gate_ups, down_weight, norm_gain, mix, outs, begun=()):
    rows = mix.shape[0]
    width = down_weight.shape[2]
    chunks = width // CHUNK
    groups = rows // 8
    vmem_spec = pl.BlockSpec(memory_space=pltpu.VMEM)
    count = len(pieces)
    in_vmem = functools.partial(pltpu.with_memory_space_constraint, memory_space=pltpu.VMEM)
    return pl.pallas_call(
        functools.partial(expert_kernel, count, outs, len(gate_ups), bool(begun)),
        in_specs=[vmem_spec] * (count + len(gate_ups) + 3 + len(begun)),
        out_specs=[vmem_spec] * (outs + 1),
        out_shape=[jax.ShapeDtypeStruct((groups // outs, 16, width // 2), jnp.bfloat16)] * outs
        + [jax.ShapeDtypeStruct((16, width // 2), jnp.float32)],
        scratch_shapes=[
            pltpu.VMEM((chunks // (2 if begun else 1), rows, CHUNK), jnp.bfloat16),
            pltpu.VMEM((rows, CHUNK), jnp.float32),
            pltpu.VMEM((rows, width // 8), jnp.float32),
            pltpu.VMEM((rows, width // 8), jnp.float32),
        ],
        compiler_params=pltpu.CompilerParams(vmem_limit_bytes=(8 if rows <= 128 else 24) * MIB),
        name="experts",
    )(
        *pieces,
        *(in_vmem(part) for part in gate_ups),
        in_vmem(down_weight),
        norm_gain.reshape(chunks, 1, CHUNK),
        mix,
        *begun,
    )


def body(
    query_heads,
    key_cache,
    value_cache,
    cache_lengths,
    out_weight,
    residual,
    norm_gain,
    expert_ids,
    route_weights,
    gate_up,
    down_weight,
):
    side = lax.axis_index("side")
    groups = lax.axis_size("grp")
    sessions, width = residual.shape
    half = sessions // 2
    rows = groups * half
    columns = width // groups
    arrays = (
        query_heads,
        key_cache,
        value_cache,
        cache_lengths,
        expert_ids,
        route_weights,
        norm_gain,
        residual,
    )
    if groups == CHIPS:
        *carried, gain = attend(groups, PLANES, *arrays)
        pieces = gather(carried)
        staged, done = stage(gate_up, pieces[9])
        y, mix, third = project(
            [p[None] for p in pieces], out_weight, gain, staged=(done, gate_up)
        )
        nears, fars = gather_pairs(y)
        *begun, fourth = near(nears, staged, gate_up, norm_gain)
        *sums, hidden = experts(
            fars, [third, fourth], down_weight, norm_gain, mix, 8, begun
        )
        mixture = scatter_sum(sums[:4], sums[4:])
    else:
        own_residual = lax.dynamic_slice_in_dim(residual, side * half, half, axis=0)
        residual_columns = lax.all_to_all(
            own_residual.reshape(half, groups, columns).transpose(1, 0, 2),
            "grp",
            split_axis=0,
            concat_axis=0,
            tiled=True,
        ).reshape(rows, columns)
        attn_out, gain = attend(groups, 0, *arrays)
        pieces = lax.all_gather(attn_out, "grp", axis=0)
        y, mix = project([pieces], out_weight, gain, residual_columns)
        y_all = lax.all_gather(y, "grp", axis=0).transpose(1, 0, 2)
        y_chunks = y_all.reshape(rows, width // CHUNK, CHUNK).transpose(1, 0, 2)
        *sums, hidden = experts([y_chunks], [gate_up[0]], down_weight, norm_gain, mix, 1)
        sent = lax.all_to_all(sums[0], "grp", split_axis=0, concat_axis=0, tiled=True)
        mixture = jnp.sum(sent.astype(jnp.float32), axis=0)
    ready = (hidden + mixture).astype(jnp.bfloat16)
    mine, other = ready[:half], ready[half:]
    other = lax.ppermute(other, "side", [(0, 1), (1, 0)])
    return jnp.where(
        side == 0, jnp.concatenate([mine, other]), jnp.concatenate([other, mine])
    )


def solution(mesh):
    return jax.shard_map(
        body,
        mesh=mesh,
        in_specs=(
            P("grp", None),
            P("grp", None, None),
            P("grp", None, None),
            P("grp"),
            P(None, "grp"),
            P("grp", None),
            P(),
            P("grp", None),
            P("grp", None),
            P("grp", None, None),
            P("grp", None, None),
        ),
        out_specs=P("grp", "side"),
        check_vma=False,
    )
```

```python
import functools

import jax
import jax.numpy as jnp
from jax import lax
from jax.experimental import pallas as pl
from jax.experimental.pallas import tpu as pltpu
from jax.sharding import PartitionSpec as P

HQ = 64
KVH = 4
HD = 128
HID = 768
TOPK = 8
CTX = 128
GROUP = HQ // KVH
EPS = 1e-06
CHUNK = 256
LANES = 128
MIB = 1 << 20


CHIPS = 16
PLANES = 4
PAIRS = ((0, 1), (2, 3))
BACK_PAIRS = ((2, 3), (0, 1))
ROUTING = LANES


def exchange(value, bits):
    return lax.ppermute(value, "grp", [(g, g ^ bits) for g in range(CHIPS)])


def piece_order(place, groups):
    if groups != CHIPS:
        return list(range(groups))
    return [place ^ n for n in range(CHIPS)]


def pair_order(place, groups, pairs):
    if groups != CHIPS:
        return list(range(groups))
    return [place ^ (4 * k + f) for pair in pairs for f in range(4) for k in pair]


def after(value, *done):
    return lax.optimization_barrier((value, *done))[0]


def gather(planes):
    own = planes[0]
    z1 = exchange(planes[1], 4)
    z2 = exchange(planes[2], 8)
    x0 = exchange(own, 1)
    y0 = exchange(own, 2)
    z3 = exchange(after(planes[3], z2), 12)
    c0 = exchange(x0, 2)
    x1 = exchange(after(x0, z1), 4)
    y1 = exchange(after(z1, z3), 2)
    x2 = exchange(after(z2, y0), 1)
    y2 = exchange(z2, 2)
    c1 = exchange(c0, 4)
    c2 = exchange(after(x2, x1, z2, z3), 2)
    x3 = exchange(after(z3, y2, x2), 1)
    y3 = exchange(z3, 2)
    c3 = exchange(after(y3, x1), 1)
    return [own, x0, y0, c0, z1, x1, y1, c1, z2, x2, y2, c2, z3, x3, y3, c3]


BY_NEXT_PLANE = (5, 7)


def gather_pairs(piece):
    column = [piece] + [exchange(piece, 4 * k) for k in range(1, PLANES)]
    near, far = (jnp.stack([column[k] for k in pair]) for pair in PAIRS)
    far = after(far, near)
    nears = [exchange(near, f) if f else near for f in range(4)]
    fars = [exchange(far, f) if f else far for f in range(4)]
    return nears, fars


def add(*terms):
    return sum(t.astype(jnp.float32) for t in terms).astype(jnp.bfloat16)


def scatter_sum(far, near):
    far = add(far[0], *[exchange(far[f], f) for f in (3, 1, 2)])
    near = add(near[0], *[exchange(near[f], f) for f in (3, 1, 2)])
    late = exchange(far[0], 8).astype(jnp.float32) + exchange(far[1], 12).astype(jnp.float32)
    late = lax.optimization_barrier(late)
    return near[0].astype(jnp.float32) + exchange(near[1], 4).astype(jnp.float32) + late


def attend_kernel(
    planes, ids_hbm, route_hbm, len_hbm, g_hbm, r_hbm, q_hbm, k_hbm, v_hbm, *refs
):
    o_refs = refs[: max(1, planes)]
    gain_ref = refs[max(1, planes)]
    o_ref = o_refs[0]
    len_ref, ids_ref, route_ref, tail_ref, r_ref, q_ref, k_ref, v_ref, sems = refs[-9:]
    side = lax.axis_index("side")
    half = k_ref.shape[0]
    rows = GROUP * half
    depth = HQ * HD // 2
    mine = [side * half + s for s in range(half)]
    small = [
        pltpu.make_async_copy(ids_hbm, ids_ref, sems.at[2 * half + 3]),
        pltpu.make_async_copy(route_hbm, route_ref, sems.at[2 * half + 4]),
    ]
    copies = [
        pltpu.make_async_copy(len_hbm, len_ref, sems.at[2 * half + 1]),
        pltpu.make_async_copy(q_hbm, q_ref, sems.at[2 * half]),
    ]
    copies += [
        pltpu.make_async_copy(k_hbm.at[mine[s]], k_ref.at[s], sems.at[s]) for s in range(half)
    ]
    late = [
        pltpu.make_async_copy(v_hbm.at[mine[s]], v_ref.at[s], sems.at[half + s])
        for s in range(half)
    ]
    late.append(pltpu.make_async_copy(r_hbm, r_ref, sems.at[2 * half + 2]))
    gain = g_hbm.at[lax.axis_index("grp")]
    late.append(pltpu.make_async_copy(gain, gain_ref, sems.at[2 * half + 5]))
    for copy in small + copies + late:
        copy.start()
    session = lax.broadcasted_iota(jnp.int32, (rows, CTX), 0) % half
    place = lax.broadcasted_iota(jnp.int32, (rows, CTX), 1)
    for copy in small:
        copy.wait()
    terms, rest = [], route_ref[...]
    for _ in range(3):
        terms.append(rest.astype(jnp.bfloat16).astype(jnp.float32))
        rest = rest - terms[-1]
    count = 2 * half
    tail_ref[...] = jnp.zeros_like(tail_ref)
    tail_ref[:, :count] = jnp.concatenate(terms[1:], axis=0)
    second = pltpu.roll(tail_ref[...], LANES // 2, axis=1)
    tail_ref[:, :count] = jnp.concatenate([ids_ref[...].astype(jnp.float32), terms[0]], axis=0)
    tail = jnp.where(
        lax.broadcasted_iota(jnp.int32, second.shape, 1) < LANES // 2, tail_ref[...], second
    ).astype(jnp.bfloat16)
    for ref in o_refs:
        ref[:, depth : depth + ROUTING] = tail

    for copy in copies:
        copy.wait()
    lives = [(session == s) & (place < len_ref[mine[s]]) for s in range(half)]
    spreads = []
    for kv in range(KVH):
        parts = []
        for h in range(kv * GROUP, (kv + 1) * GROUP):
            both = q_ref[:, h * HD : (h + 1) * HD].astype(jnp.float32)
            parts.append(jnp.where(side == 0, both[:half], both[half:]))
        queries = jnp.concatenate(parts, axis=0).astype(jnp.bfloat16)
        keys = k_ref[:, :, kv * HD : (kv + 1) * HD].reshape(half * CTX, HD)
        every = lax.dot_general(
            queries, keys, (((1,), (1,)), ((), ())), preferred_element_type=jnp.float32
        )
        scores = jnp.full((rows, CTX), -1e30, jnp.float32)
        for s in range(half):
            part = every[:, s * CTX : (s + 1) * CTX] * HD ** (-0.5)
            scores = jnp.where(lives[s], part, scores)
        lifted = jnp.exp(scores - jnp.max(scores, axis=-1, keepdims=True))
        weights = lifted / jnp.sum(lifted, axis=-1, keepdims=True)
        spreads.append(
            jnp.concatenate(
                [jnp.where(session == s, weights, 0.0).astype(jnp.bfloat16) for s in range(half)],
                axis=1,
            )
        )
    for copy in late:
        copy.wait()
    outs = []
    for kv in range(KVH):
        values = v_ref[:, :, kv * HD : (kv + 1) * HD].reshape(half * CTX, HD)
        outs.append(jnp.dot(spreads[kv], values, preferred_element_type=jnp.float32))
    later = KVH // 2
    for kv in range(later):
        for h in range(GROUP):
            pair = [out[h * half : (h + 1) * half] for out in (outs[kv], outs[kv + later])]
            both = jnp.concatenate(pair, axis=0).astype(jnp.bfloat16)
            for ref in o_refs:
                ref[:, (kv * GROUP + h) * HD : (kv * GROUP + h + 1) * HD] = both
    here = lax.axis_index("grp") // 4
    for k in range(planes):
        wide = r_ref.shape[1] // planes // 2
        parts = []
        for part in range(2):
            start = pl.multiple_of(((here ^ k) * 2 + part) * wide, wide)
            both = r_ref[:, pl.ds(start, wide)].astype(jnp.float32)
            parts.append(jnp.where(side == 0, both[:half], both[half:]))
        tail = jnp.concatenate(parts, axis=0).astype(jnp.bfloat16)
        o_refs[k][:, depth + ROUTING : depth + ROUTING + wide] = tail
        if k == 1:
            o_ref[:, depth + ROUTING + wide :] = tail


def attend(
    groups,
    planes,
    query_heads,
    key_cache,
    value_cache,
    cache_lengths,
    expert_ids,
    route_weights,
    norm_gain,
    residual,
):
    sessions, width = residual.shape
    half = sessions // 2
    columns = width // groups
    hbm_spec = pl.BlockSpec(memory_space=pltpu.HBM)
    vmem_spec = pl.BlockSpec(memory_space=pltpu.VMEM)
    in_hbm = functools.partial(pltpu.with_memory_space_constraint, memory_space=pltpu.HBM)
    outs = max(1, planes)
    tail = width // planes // 2 if planes else 0
    carried = [HQ * HD // 2 + ROUTING + tail * (2 if k == 0 else 1) for k in range(outs)]
    return pl.pallas_call(
        functools.partial(attend_kernel, planes),
        in_specs=[hbm_spec] * 8,
        out_specs=[vmem_spec] * (outs + 1),
        out_shape=[jax.ShapeDtypeStruct((sessions, n), jnp.bfloat16) for n in carried]
        + [jax.ShapeDtypeStruct((1, columns), jnp.float32)],
        scratch_shapes=[
            pltpu.SMEM((sessions,), jnp.int32),
            pltpu.VMEM((TOPK, sessions), jnp.int32),
            pltpu.VMEM((TOPK, sessions), jnp.float32),
            pltpu.VMEM((sessions, ROUTING), jnp.float32),
            pltpu.VMEM((sessions, width), jnp.bfloat16),
            pltpu.VMEM((sessions, HQ * HD), jnp.bfloat16),
            pltpu.VMEM((half, CTX, KVH * HD), jnp.bfloat16),
            pltpu.VMEM((half, CTX, KVH * HD), jnp.bfloat16),
            pltpu.SemaphoreType.DMA((2 * half + 6,)),
        ],
        compiler_params=pltpu.CompilerParams(vmem_limit_bytes=8 * MIB),
        name="attend",
    )(
        in_hbm(expert_ids.T),
        in_hbm(route_weights.T),
        in_hbm(cache_lengths),
        in_hbm(norm_gain.reshape(groups, 1, columns)),
        in_hbm(residual),
        in_hbm(query_heads),
        in_hbm(key_cache),
        in_hbm(value_cache),
    )


def project_kernel(count, waits, *refs):
    refs = refs[waits:]
    pieces = refs[:count]
    *rest, w_ref, g_ref, y_ref, mix_ref, plain = refs[count:]
    blocks, sessions, _ = pieces[0].shape
    depth = w_ref.shape[0] // 2
    half = sessions // 2
    columns = w_ref.shape[1]
    groups = count * blocks
    side, place = lax.axis_index("side"), lax.axis_index("grp")
    order = piece_order(place, groups)
    total = None
    for part in range(2):
        chunk = depth // 4
        for j in range(4):
            a = jnp.concatenate(
                [
                    piece[:, :, j * chunk : (j + 1) * chunk].reshape(blocks * sessions, chunk)
                    for piece in pieces
                ],
                axis=0,
            )
            start = part * depth + j * chunk
            term = jnp.dot(a, w_ref[start : start + chunk], preferred_element_type=jnp.float32)
            got = term if j == 0 else got + term
        got = got.reshape(groups, 2, half, columns)[:, part]
        total = got if total is None else total + got
    own = lax.broadcasted_iota(jnp.int32, (half, LANES), 1) == side * half + (
        lax.broadcasted_iota(jnp.int32, (half, LANES), 0)
    )
    for n in range(count):
        for b in range(blocks):
            span = pl.ds(pl.multiple_of(order[n * blocks + b] * half, half), half)
            value = total[n * blocks + b]
            if not rest:
                start = depth + ROUTING + (2 * columns if n in BY_NEXT_PLANE else 0)
                tail = pieces[n][b, :, start : start + 2 * columns].astype(jnp.float32)
                spot = place % 4
                tail = jnp.where(spot // 2 == 0, tail[:half], tail[half:])
                value = value + jnp.where(spot % 2 == 0, tail[:, :columns], tail[:, columns:])
            plain[span, :] = value
            first = pieces[n][b, :, depth : depth + ROUTING].astype(jnp.float32)
            second = pltpu.roll(first, LANES // 2, axis=1)
            weights = first[half:] + (second[:half] + second[half:])
            chosen = jnp.where(first[:half] == place.astype(jnp.float32), weights, 0.0)
            chosen = jnp.sum(chosen, axis=0, keepdims=True)
            mix_ref[span, :] = jnp.sum(jnp.where(own, chosen, 0.0), axis=1, keepdims=True)
    hidden = plain[...]
    if rest:
        hidden = hidden + rest[0][...].astype(jnp.float32)
    y_ref[...] = (hidden * g_ref[...]).astype(jnp.bfloat16)


def project(pieces, out_weight, gain_columns, residual_columns=None, waits=()):
    count = len(pieces)
    columns = out_weight.shape[1]
    rows = sum(p.shape[0] for p in pieces) * pieces[0].shape[1] // 2
    rest = [] if residual_columns is None else [residual_columns]
    vmem_spec = pl.BlockSpec(memory_space=pltpu.VMEM)
    return pl.pallas_call(
        functools.partial(project_kernel, count, len(waits)),
        in_specs=[pl.BlockSpec(memory_space=pl.ANY)] * len(waits)
        + [vmem_spec] * (count + len(rest) + 2),
        out_specs=[vmem_spec] * 2,
        out_shape=[
            jax.ShapeDtypeStruct((rows, columns), jnp.bfloat16),
            jax.ShapeDtypeStruct((rows, 1), jnp.float32),
        ],
        scratch_shapes=[pltpu.VMEM((rows, columns), jnp.float32)],
        compiler_params=pltpu.CompilerParams(vmem_limit_bytes=8 * MIB),
        name="project",
    )(
        *waits,
        *pieces,
        *rest,
        pltpu.with_memory_space_constraint(out_weight, pltpu.VMEM),
        gain_columns,
    )


def take_chunk(store, g_ref, plain, hid_ref, chunk, chunks):
    side, place = lax.axis_index("side"), lax.axis_index("grp")
    value = store.astype(jnp.float32) * (1.0 / g_ref[chunk])
    plain[...] = value
    local, late = chunk % (chunks // 2), chunk // (chunks // 2)
    rows = pl.ds(pl.multiple_of(8 * ((side + late) % 2), 8), 8)
    columns = pl.ds(pl.multiple_of(local * CHUNK, CHUNK), CHUNK)
    hid_ref[rows, columns] = plain[pl.ds(pl.multiple_of(place * 8, 8), 8), :]
    squares = value * value
    return squares[:, :LANES] + squares[:, LANES:]


def weight_copies(gu_hbm, dst, sems, first):
    return [
        pltpu.make_async_copy(
            gu_hbm.at[0, pl.ds(pl.multiple_of((first + j) * CHUNK, CHUNK), CHUNK)],
            dst.at[pl.ds(j * CHUNK, CHUNK)],
            sems.at[j],
        )
        for j in range(dst.shape[0] // CHUNK)
    ]


def first_chunk(half, chunks):
    return ((lax.axis_index("grp") // (CHIPS // 2)) ^ half) * (chunks // 2)


def stage_kernel(_, gu_hbm, weights, quarter, done, sems, quarter_sems):
    chunks = gu_hbm.shape[1] // CHUNK
    copies = weight_copies(gu_hbm, weights, sems, first_chunk(0, chunks))
    copies += weight_copies(gu_hbm, quarter, quarter_sems, first_chunk(1, chunks))
    for copy in copies:
        copy.start()
    done[...] = jnp.zeros_like(done)
    for copy in copies:
        copy.wait()


def stage(gate_up, arrived):
    depth = gate_up.shape[1] // 2
    hbm_spec = pl.BlockSpec(memory_space=pltpu.HBM)
    vmem_spec = pl.BlockSpec(memory_space=pltpu.VMEM)
    return pl.pallas_call(
        stage_kernel,
        in_specs=[pl.BlockSpec(memory_space=pl.ANY), hbm_spec],
        out_specs=[vmem_spec] * 3,
        out_shape=[
            jax.ShapeDtypeStruct((depth, 2 * HID), jnp.bfloat16),
            jax.ShapeDtypeStruct((depth // 2, 2 * HID), jnp.bfloat16),
            jax.ShapeDtypeStruct((8, LANES), jnp.float32),
        ],
        scratch_shapes=[
            pltpu.SemaphoreType.DMA((depth // CHUNK,)),
            pltpu.SemaphoreType.DMA((depth // 2 // CHUNK,)),
        ],
        compiler_params=pltpu.CompilerParams(vmem_limit_bytes=2 * MIB),
        cost_estimate=pl.CostEstimate(
            flops=0, bytes_accessed=depth * 6 * HID, transcendentals=0
        ),
        name="stage",
    )(arrived, pltpu.with_memory_space_constraint(gate_up, pltpu.HBM))


def near_kernel(count, *refs):
    pieces = refs[:count]
    weights, gu_hbm, g_ref, acc, sq_ref, hid_ref, quarter, store, plain, sems = refs[count:]
    chunks = g_ref.shape[0]
    own = chunks // 2
    copies = weight_copies(gu_hbm, quarter, sems, first_chunk(1, chunks) + own // 2)
    for copy in copies:
        copy.start()
    order = pair_order(lax.axis_index("grp"), CHIPS, PAIRS)[:own]
    squares = jnp.zeros(sq_ref.shape, jnp.float32)
    for n in range(count):
        for b in range(2):
            chunk = order[2 * n + b]
            piece = pieces[n][b]
            store[chunk - first_chunk(0, chunks)] = piece
            squares += take_chunk(piece, g_ref, plain, hid_ref, chunk, chunks)
    sq_ref[...] = squares
    y = jnp.concatenate([store[j] for j in range(own)], axis=1)
    for n in range(2 * HID // CHUNK):
        cols = slice(n * CHUNK, (n + 1) * CHUNK)
        acc[:, cols] = jnp.dot(y, weights[:, cols], preferred_element_type=jnp.float32)
    for copy in copies:
        copy.wait()


def near(pieces, staged, gate_up, norm_gain):
    rows = pieces[0].shape[1]
    width = gate_up.shape[1]
    chunks = width // CHUNK
    vmem_spec = pl.BlockSpec(memory_space=pltpu.VMEM)
    count = len(pieces)
    return pl.pallas_call(
        functools.partial(near_kernel, count),
        in_specs=[vmem_spec] * (count + 1) + [pl.BlockSpec(memory_space=pltpu.HBM), vmem_spec],
        out_specs=[vmem_spec] * 4,
        out_shape=[
            jax.ShapeDtypeStruct((rows, 2 * HID), jnp.float32),
            jax.ShapeDtypeStruct((rows, LANES), jnp.float32),
            jax.ShapeDtypeStruct((16, width // 2), jnp.float32),
            jax.ShapeDtypeStruct((width // 4, 2 * HID), jnp.bfloat16),
        ],
        scratch_shapes=[
            pltpu.VMEM((chunks // 2, rows, CHUNK), jnp.bfloat16),
            pltpu.VMEM((rows, CHUNK), jnp.float32),
            pltpu.SemaphoreType.DMA((chunks // 4,)),
        ],
        compiler_params=pltpu.CompilerParams(vmem_limit_bytes=6 * MIB),
        cost_estimate=pl.CostEstimate(
            flops=2 * rows * width * HID, bytes_accessed=width * 4 * HID, transcendentals=0
        ),
        name="near",
    )(
        *pieces,
        pltpu.with_memory_space_constraint(staged, pltpu.VMEM),
        pltpu.with_memory_space_constraint(gate_up, pltpu.HBM),
        norm_gain.reshape(chunks, 1, CHUNK),
    )


def expert_kernel(count, outs, parts, resumed, *refs):
    pieces = refs[:count]
    gu_refs = refs[count : count + parts]
    dn_ref, g_ref, mix_ref, *rest = refs[count + parts :]
    if resumed:
        acc_ref, sq_ref, old_ref = rest[:3]
        rest = rest[3:]
    o_refs, (hid_ref, store, plain, first, second) = rest[:outs], rest[outs:]
    side, place = lax.axis_index("side"), lax.axis_index("grp")
    own, rows, _ = store.shape
    chunks = g_ref.shape[0]
    width = chunks * CHUNK
    groups = rows // 8
    blocks = groups // outs
    spans = pieces[0].shape[0]
    back = pair_order(place, groups, BACK_PAIRS)
    if resumed:
        order = pair_order(place, groups, PAIRS)[own:]
        base = first_chunk(1, chunks)
        squares = sq_ref[...]
        hid_ref[...] = old_ref[...]
    else:
        order, base = list(range(chunks)), 0
        squares = jnp.zeros((rows, LANES), jnp.float32)
    for n in range(count):
        for b in range(spans):
            chunk = order[n * spans + b]
            piece = pieces[n][b]
            store[chunk - base] = piece
            squares += take_chunk(piece, g_ref, plain, hid_ref, chunk, chunks)
    mean = jnp.sum(squares, axis=-1, keepdims=True) * (1.0 / width)
    scaling = lax.rsqrt(mean + EPS)
    span = own // parts
    ys = [
        jnp.concatenate([store[p * span + j] for j in range(span)], axis=1) for p in range(parts)
    ]
    activated = []
    for n in range(HID // CHUNK):
        halves = []
        for start in (0, HID):
            cols = slice(start + n * CHUNK, start + (n + 1) * CHUNK)
            value = sum(
                jnp.dot(y, gu_ref[:, cols], preferred_element_type=jnp.float32)
                for y, gu_ref in zip(ys, gu_refs)
            )
            if resumed:
                value = value + acc_ref[:, cols]
            halves.append(value * scaling)
        gate, up = halves
        activated.append((gate / (1.0 + jnp.exp(-gate)) * up).astype(jnp.bfloat16))
    activated = jnp.concatenate(activated, axis=1)
    mix = mix_ref[...]
    wide = width // 8
    for j in range(4):
        results = [
            jnp.dot(
                activated,
                dn_ref[0, :, start + j * wide : start + (j + 1) * wide],
                preferred_element_type=jnp.float32,
            )
            * mix
            for start in (0, width // 2)
        ]
        first[...] = jnp.where(side == 0, results[0], results[1])
        second[...] = jnp.where(side == 0, results[1], results[0])
        for n in range(outs):
            for b in range(blocks):
                span = pl.ds(pl.multiple_of(back[n * blocks + b] * 8, 8), 8)
                o_refs[n][b, :, j * wide : (j + 1) * wide] = jnp.concatenate(
                    [first[span, :], second[span, :]], axis=0
                ).astype(jnp.bfloat16)


def experts(pieces, gate_ups, down_weight, norm_gain, mix, outs, begun=()):
    rows = mix.shape[0]
    width = down_weight.shape[2]
    chunks = width // CHUNK
    groups = rows // 8
    vmem_spec = pl.BlockSpec(memory_space=pltpu.VMEM)
    count = len(pieces)
    in_vmem = functools.partial(pltpu.with_memory_space_constraint, memory_space=pltpu.VMEM)
    return pl.pallas_call(
        functools.partial(expert_kernel, count, outs, len(gate_ups), bool(begun)),
        in_specs=[vmem_spec] * (count + len(gate_ups) + 3 + len(begun)),
        out_specs=[vmem_spec] * (outs + 1),
        out_shape=[jax.ShapeDtypeStruct((groups // outs, 16, width // 2), jnp.bfloat16)] * outs
        + [jax.ShapeDtypeStruct((16, width // 2), jnp.float32)],
        scratch_shapes=[
            pltpu.VMEM((chunks // (2 if begun else 1), rows, CHUNK), jnp.bfloat16),
            pltpu.VMEM((rows, CHUNK), jnp.float32),
            pltpu.VMEM((rows, width // 8), jnp.float32),
            pltpu.VMEM((rows, width // 8), jnp.float32),
        ],
        compiler_params=pltpu.CompilerParams(vmem_limit_bytes=(8 if rows <= 128 else 24) * MIB),
        name="experts",
    )(
        *pieces,
        *(in_vmem(part) for part in gate_ups),
        in_vmem(down_weight),
        norm_gain.reshape(chunks, 1, CHUNK),
        mix,
        *begun,
    )


def body(
    query_heads,
    key_cache,
    value_cache,
    cache_lengths,
    out_weight,
    residual,
    norm_gain,
    expert_ids,
    route_weights,
    gate_up,
    down_weight,
):
    side = lax.axis_index("side")
    groups = lax.axis_size("grp")
    sessions, width = residual.shape
    half = sessions // 2
    rows = groups * half
    columns = width // groups
    arrays = (
        query_heads,
        key_cache,
        value_cache,
        cache_lengths,
        expert_ids,
        route_weights,
        norm_gain,
        residual,
    )
    if groups == CHIPS:
        *carried, gain = attend(groups, PLANES, *arrays)
        pieces = gather(carried)
        staged, third, done = stage(gate_up, pieces[9])
        y, mix = project([p[None] for p in pieces], out_weight, gain, waits=(done,))
        nears, fars = gather_pairs(y)
        *begun, fourth = near(nears, staged, gate_up, norm_gain)
        *sums, hidden = experts(
            fars, [third, fourth], down_weight, norm_gain, mix, 8, begun
        )
        mixture = scatter_sum(sums[:4], sums[4:])
    else:
        own_residual = lax.dynamic_slice_in_dim(residual, side * half, half, axis=0)
        residual_columns = lax.all_to_all(
            own_residual.reshape(half, groups, columns).transpose(1, 0, 2),
            "grp",
            split_axis=0,
            concat_axis=0,
            tiled=True,
        ).reshape(rows, columns)
        attn_out, gain = attend(groups, 0, *arrays)
        pieces = lax.all_gather(attn_out, "grp", axis=0)
        y, mix = project([pieces], out_weight, gain, residual_columns)
        y_all = lax.all_gather(y, "grp", axis=0).transpose(1, 0, 2)
        y_chunks = y_all.reshape(rows, width // CHUNK, CHUNK).transpose(1, 0, 2)
        *sums, hidden = experts([y_chunks], [gate_up[0]], down_weight, norm_gain, mix, 1)
        sent = lax.all_to_all(sums[0], "grp", split_axis=0, concat_axis=0, tiled=True)
        mixture = jnp.sum(sent.astype(jnp.float32), axis=0)
    ready = (hidden + mixture).astype(jnp.bfloat16)
    mine, other = ready[:half], ready[half:]
    other = lax.ppermute(other, "side", [(0, 1), (1, 0)])
    return jnp.where(
        side == 0, jnp.concatenate([mine, other]), jnp.concatenate([other, mine])
    )


def solution(mesh):
    return jax.shard_map(
        body,
        mesh=mesh,
        in_specs=(
            P("grp", None),
            P("grp", None, None),
            P("grp", None, None),
            P("grp"),
            P(None, "grp"),
            P("grp", None),
            P(),
            P("grp", None),
            P("grp", None),
            P("grp", None, None),
            P("grp", None, None),
        ),
        out_specs=P("grp", "side"),
        check_vma=False,
    )
```
